256 devices in a mesh: row: 8 (over y, x_hi), col: 32 (over x_lo, z, core).
Axes of the slice: x: 4 (x_hi: 2, x_lo: 2; x = x_hi * 2 + x_lo), y: 4, z: 8, core: 2. Of those that a mesh axis runs over, the one named last changes fastest.
Arguments:
- pair: bfloat16 [1024, 1024, 128], P('row', 'col'), may hold values from -6 to 6
- layernorm_gain: float32 [128], replicated, may hold values from 0.25 to 1.75
- layernorm_bias: float32 [128], replicated, may hold values from -3 to 3
- proj_weight: bfloat16 [128, 512], replicated, may hold values from -0.5 to 0.5
- product_grad: bfloat16 [1024, 1024, 128], P('row', 'col'), may hold values from -0.1875 to 0.1875
Outputs:
- pairwise_gradient: bfloat16 [1024, 1024, 128], P('row', 'col')
- proj_grad: float32 [128, 512], replicated
- layernorm_gradient: float32 [2, 128], replicated
The draws below stay inside these ranges and needn't reach their ends.
All inputs are finite; a program needn't handle non-finite values.
Results may differ from the reference program's by a relative error of at most 0.0072.
Values may be sent and summed in bfloat16 or wider, within the bound.
No kernel may reach another device: no remote copies, remote signals or barrier semaphores. Data moves between devices by JAX's collectives and lax.ppermute only.
A program may use at most 128 MiB of HBM per device.

```python
import jax
import jax.numpy as jnp
from jax import lax

C = 128
H = 128
RESIDUE_COUNT = 1024


def level_of(key, dims, pieces, low, largest):
    level = 1.0
    for axis_at, blocks in pieces:
        draws = jax.random.uniform(jax.random.fold_in(jax.random.fold_in(key, 6), axis_at), (blocks,), jnp.float32, low / len(pieces), largest / len(pieces))
        level = level * jnp.repeat(jnp.exp(draws), dims[axis_at] // blocks).reshape((-1,) + (1,) * (len(dims) - 1 - axis_at))
    return level


def bell_draw(key, dims, deviation, bound, split=(), held_as=jnp.bfloat16):
    gain = level_of(key, dims, split, -0.22, 0.18) if split else 1.0
    drawn = jax.random.normal(key, dims, jnp.float32) * deviation * gain
    return jnp.minimum(jnp.maximum(drawn, -bound), bound).astype(held_as)


def setup_inputs(seed: int = 0) -> dict:
    key_list = jax.random.split(jax.random.key(seed), 6)
    pair = bell_draw(key_list[0], (RESIDUE_COUNT, RESIDUE_COUNT, C), 1.0, 6.0, ((0, 8), (1, 32)))
    layernorm_gain = jnp.clip(1.0 + 0.15 * jax.random.normal(key_list[1], (C,), jnp.float32), 0.25, 1.75)
    layernorm_bias = bell_draw(key_list[2], (C,), 0.5, 3.0, (), jnp.float32)
    proj_weight = bell_draw(key_list[3], (C, 4 * H), C ** -0.5, 0.5)
    product_grad = bell_draw(key_list[4], (RESIDUE_COUNT, RESIDUE_COUNT, H), RESIDUE_COUNT ** -0.5, 0.1875, ((0, 8), (1, 32)))
    return {"pair": pair, "layernorm_gain": layernorm_gain, "layernorm_bias": layernorm_bias, "proj_weight": proj_weight, "product_grad": product_grad}


def reference(pair, layernorm_gain, layernorm_bias, proj_weight, product_grad):
    flat = pair.reshape(RESIDUE_COUNT * RESIDUE_COUNT, C).astype(jnp.float32)
    row_mean = lax.optimization_barrier(jnp.mean(flat, axis=1, keepdims=True))
    centred_input = flat - row_mean
    inverse_deviation = lax.rsqrt(lax.optimization_barrier(jnp.mean(centred_input * centred_input, axis=1, keepdims=True)) + 1e-05)
    standardized_input = centred_input * inverse_deviation
    normalized_input = (standardized_input * layernorm_gain + layernorm_bias).astype(jnp.bfloat16)
    proj = jnp.dot(normalized_input, proj_weight, preferred_element_type=jnp.float32)
    pa, ga, pb, gb = (proj[:, :H], proj[:, H:2 * H], proj[:, 2 * H:3 * H], proj[:, 3 * H:])
    sa = jax.nn.sigmoid(ga)
    sb = jax.nn.sigmoid(gb)
    left = (sa * pa).astype(jnp.bfloat16).reshape(RESIDUE_COUNT, RESIDUE_COUNT, H)
    right = (sb * pb).astype(jnp.bfloat16).reshape(RESIDUE_COUNT, RESIDUE_COUNT, H)

    def channel(items):
        grad_h, left_h, right_h = items
        first = jnp.dot(grad_h, right_h, preferred_element_type=jnp.float32)
        second = jnp.dot(grad_h.T, left_h, preferred_element_type=jnp.float32)
        return (first.astype(jnp.bfloat16), second.astype(jnp.bfloat16))
    left_grad, right_grad = lax.map(channel, (jnp.transpose(product_grad, (2, 0, 1)), jnp.transpose(left, (2, 0, 1)), jnp.transpose(right, (2, 0, 1))))
    left_grad = jnp.transpose(left_grad, (1, 2, 0)).reshape(RESIDUE_COUNT * RESIDUE_COUNT, H).astype(jnp.float32)
    right_grad = jnp.transpose(right_grad, (1, 2, 0)).reshape(RESIDUE_COUNT * RESIDUE_COUNT, H).astype(jnp.float32)
    dproj = jnp.concatenate([left_grad * sa, left_grad * pa * sa * (1.0 - sa), right_grad * sb, right_grad * pb * sb * (1.0 - sb)], axis=1).astype(jnp.bfloat16)
    normalized_gradient = jnp.dot(dproj, proj_weight.T, preferred_element_type=jnp.float32)
    proj_grad = jnp.dot(normalized_input.T, dproj, preferred_element_type=jnp.float32) / RESIDUE_COUNT
    layernorm_gradient = jnp.stack([lax.optimization_barrier(jnp.sum(normalized_gradient * standardized_input, axis=0)), lax.optimization_barrier(jnp.sum(normalized_gradient, axis=0))]) / RESIDUE_COUNT
    scaled_input = normalized_gradient * layernorm_gain
    pairwise_gradient = (scaled_input - lax.optimization_barrier(jnp.mean(scaled_input, axis=1, keepdims=True)) - standardized_input * lax.optimization_barrier(jnp.mean(scaled_input * standardized_input, axis=1, keepdims=True))) * inverse_deviation
    return (pairwise_gradient.astype(jnp.bfloat16).reshape(RESIDUE_COUNT, RESIDUE_COUNT, C), proj_grad, layernorm_gradient)
```

```python
import functools

import jax
import jax.numpy as jnp
from jax import lax
from jax.experimental import pallas as pl
from jax.experimental.pallas import tpu as pltpu
from jax.sharding import Mesh, PartitionSpec as P

PLANE = ("y", "xh", "xl", "c")
GROUPS = 32
SLABS = 8
STEP_ROWS = 16
VMEM_LIMIT = 48 * 1024 * 1024


def all_to_all(x, axes):
    return lax.all_to_all(x, axes, split_axis=0, concat_axis=0, tiled=True)


def shift(x, by):
    return lax.ppermute(x, "z", [(i, (i + by) % SLABS) for i in range(SLABS)])


def normalize(pair_ref, gain_ref, bias_ref):
    x = pair_ref[...].astype(jnp.float32)
    x = x.reshape(x.shape[0] * x.shape[1], x.shape[2])
    centred = x - jnp.mean(x, axis=1, keepdims=True)
    inverse = lax.rsqrt(jnp.mean(centred * centred, axis=1, keepdims=True) + 1e-05)
    xhat = centred * inverse
    normed = (xhat * gain_ref[...] + bias_ref[...]).astype(jnp.bfloat16)
    return xhat, inverse, normed


def project(normed, weight_ref):
    proj = jnp.dot(normed, weight_ref[...], preferred_element_type=jnp.float32)
    h = proj.shape[1] // 4
    return proj[:, :h], proj[:, h : 2 * h], proj[:, 2 * h : 3 * h], proj[:, 3 * h :]


def pre_kernel(pair_ref, gain_ref, bias_ref, weight_ref, left_ref, right_ref):
    _, _, normed = normalize(pair_ref, gain_ref, bias_ref)
    pa, ga, pb, gb = project(normed, weight_ref)
    left_ref[...] = (jax.nn.sigmoid(ga) * pa).astype(jnp.bfloat16).reshape(left_ref.shape)
    right_ref[...] = (jax.nn.sigmoid(gb) * pb).astype(jnp.bfloat16).reshape(right_ref.shape)


def pre(pair, gain, bias, weight):
    rows, cols, width = pair.shape
    tile = pl.BlockSpec((STEP_ROWS, cols, width), lambda i: (i, 0, 0))
    whole = lambda *shape: pl.BlockSpec(shape, lambda i: (0,) * len(shape))
    return pl.pallas_call(
        pre_kernel,
        grid=(rows // STEP_ROWS,),
        in_specs=[tile, whole(1, width), whole(1, width), whole(*weight.shape)],
        out_specs=[tile, tile],
        out_shape=[jax.ShapeDtypeStruct(pair.shape, jnp.bfloat16)] * 2,
        compiler_params=pltpu.CompilerParams(vmem_limit_bytes=VMEM_LIMIT),
        cost_estimate=pl.CostEstimate(
            flops=2 * rows * cols * width * 512, bytes_accessed=3 << 20, transcendentals=1 << 20
        ),
        name="gated_projections",
    )(pair, gain, bias, weight)


def post_kernel(
    pair_ref, left_ref, right_ref, gain_ref, bias_ref, weight_ref, weight_t_ref, grad_ref, total_ref
):
    step = pl.program_id(0)

    @pl.when(step == 0)
    def _():
        total_ref[...] = jnp.zeros_like(total_ref)

    xhat, inverse, normed = normalize(pair_ref, gain_ref, bias_ref)
    pa, ga, pb, gb = project(normed, weight_ref)
    width = xhat.shape[1]
    left = left_ref[...].astype(jnp.float32).reshape(xhat.shape)
    right = right_ref[...].astype(jnp.float32).reshape(xhat.shape)
    sa = jax.nn.sigmoid(ga)
    sb = jax.nn.sigmoid(gb)
    la = left * sa
    rb = right * sb
    dproj = jnp.concatenate(
        [
            la.astype(jnp.bfloat16),
            (la * pa * (1.0 - sa)).astype(jnp.bfloat16),
            rb.astype(jnp.bfloat16),
            (rb * pb * (1.0 - sb)).astype(jnp.bfloat16),
        ],
        axis=1,
    )
    dnormed = jnp.dot(dproj, weight_t_ref[...], preferred_element_type=jnp.float32)
    wgrad = lax.dot_general(
        normed, dproj, (((0,), (0,)), ((), ())), preferred_element_type=jnp.float32
    )
    for block in range(4):
        total_ref[block * width : (block + 1) * width, :] += wgrad[
            :, block * width : (block + 1) * width
        ]
    total_ref[4 * width : 4 * width + 1, :] += jnp.sum(dnormed * xhat, axis=0, keepdims=True)
    total_ref[4 * width + 8 : 4 * width + 9, :] += jnp.sum(dnormed, axis=0, keepdims=True)
    g = dnormed * gain_ref[...]
    grad = (
        g
        - jnp.mean(g, axis=1, keepdims=True)
        - xhat * jnp.mean(g * xhat, axis=1, keepdims=True)
    ) * inverse
    grad_ref[...] = grad.astype(jnp.bfloat16).reshape(grad_ref.shape)


def post(pair, left, right, gain, bias, weight, total_rows):
    rows, cols, width = pair.shape
    tile = pl.BlockSpec((STEP_ROWS, cols, width), lambda i: (i, 0, 0))
    whole = lambda *shape: pl.BlockSpec(shape, lambda i: (0,) * len(shape))
    return pl.pallas_call(
        post_kernel,
        grid=(rows // STEP_ROWS,),
        in_specs=[
            tile,
            tile,
            tile,
            whole(1, width),
            whole(1, width),
            whole(*weight.shape),
            whole(*weight.shape[::-1]),
        ],
        out_specs=[tile, whole(total_rows, width)],
        out_shape=[
            jax.ShapeDtypeStruct(pair.shape, jnp.bfloat16),
            jax.ShapeDtypeStruct((total_rows, width), jnp.float32),
        ],
        compiler_params=pltpu.CompilerParams(vmem_limit_bytes=VMEM_LIMIT),
        cost_estimate=pl.CostEstimate(
            flops=6 * rows * cols * width * 512, bytes_accessed=5 << 20, transcendentals=1 << 20
        ),
        name="input_gradients",
    )(pair, left, right, gain, bias, weight, weight.T)


def assemble(refs):
    pieces = [piece for ref in refs for piece in ref[:, 0]]
    across = [
        jnp.concatenate(pieces[4 * r : 4 * r + 4], axis=0) for r in range(len(pieces) // 4)
    ]
    return jnp.concatenate(across, axis=1)


def halves(a, b):
    return (
        jnp.concatenate([a[:, :64], b[:, :64]], axis=1),
        jnp.concatenate([a[:, 64:], b[:, 64:]], axis=1),
    )


def product_kernel(offsets, n_refs, finish, with_sums, slab_ref, left_ref, right_ref, *refs):
    block_refs = refs[:n_refs]
    rest = refs[n_refs:]
    if with_sums:
        sum_in, second_in, *rest = rest
    if finish:
        out_ref, by_slab, second = rest
    else:
        sum_out, second_out, by_slab, second = rest
    slab = slab_ref[0]
    left = assemble([left_ref])
    right = assemble([right_ref])
    for m in range(4):
        even, odd = halves(
            right[:, 128 * m : 128 * m + 128], right[:, 512 + 128 * m : 640 + 128 * m]
        )
        by_slab[2 * m] = even
        by_slab[2 * m + 1] = odd
    total = None
    if with_sums:
        total = sum_in[0]
        second[...] = second_in[0]
    at = 0
    for offset, parts in offsets:
        block = assemble(block_refs[at : at + parts])
        at += parts
        where = lax.rem(slab + offset, SLABS)
        term = jnp.dot(by_slab[where], block, preferred_element_type=jnp.float32)
        total = term if total is None else total + term
        second[where] = lax.dot_general(
            left, block, (((1,), (1,)), ((), ())), preferred_element_type=jnp.float32
        ).astype(jnp.bfloat16)
    if not finish:
        sum_out[0] = total
        second_out[0] = second[...]
        return
    first = total.astype(jnp.bfloat16)
    for r in range(8):
        for c in range(4):
            out_ref[4 * r + c, 0, 0] = first[32 * c : 32 * c + 32, 128 * r : 128 * r + 128]
    for m in range(4):
        low, high = halves(second[2 * m], second[2 * m + 1])
        for c in range(4):
            out_ref[4 * m + c, 1, 0] = low[32 * c : 32 * c + 32]
            out_ref[4 * (m + 4) + c, 1, 0] = high[32 * c : 32 * c + 32]


def products(slab, left, right, blocks, sums, finish):
    groups, channels, depth, width = left.shape
    arrays = [a for _, parts in blocks for a in parts]
    piece = lambda a: pl.BlockSpec((a.shape[0], 1, depth, width), lambda h: (0, h, 0, 0))
    sum_specs = [
        pl.BlockSpec((1, 128, 1024), lambda h: (h, 0, 0)),
        pl.BlockSpec((1, SLABS, 128, 128), lambda h: (h, 0, 0, 0)),
    ]
    sum_shapes = [
        jax.ShapeDtypeStruct((channels, 128, 1024), jnp.float32),
        jax.ShapeDtypeStruct((channels, SLABS, 128, 128), jnp.bfloat16),
    ]
    operands = [slab, left, right, *arrays] + (list(sums) if sums else [])
    aliases = {}
    if finish:
        out_specs = pl.BlockSpec((groups, 2, 1, depth, width), lambda h: (0, 0, h, 0, 0))
        out_shape = jax.ShapeDtypeStruct((groups, 2, channels, depth, width), jnp.bfloat16)
    else:
        out_specs, out_shape = sum_specs, sum_shapes
        if sums:
            aliases = {len(operands) - 2: 0, len(operands) - 1: 1}
    kernel = functools.partial(
        product_kernel,
        [(offset, len(parts)) for offset, parts in blocks],
        len(arrays),
        finish,
        bool(sums),
    )
    return pl.pallas_call(
        kernel,
        grid=(channels,),
        in_specs=[pl.BlockSpec(memory_space=pltpu.SMEM), piece(left), piece(right)]
        + [piece(a) for a in arrays]
        + (sum_specs if sums else []),
        out_specs=out_specs,
        out_shape=out_shape,
        scratch_shapes=[
            pltpu.VMEM((SLABS, 128, 128), jnp.bfloat16),
            pltpu.VMEM((SLABS, 128, 128), jnp.bfloat16),
        ],
        input_output_aliases=aliases,
        compiler_params=pltpu.CompilerParams(vmem_limit_bytes=VMEM_LIMIT),
        cost_estimate=pl.CostEstimate(
            flops=4 * channels * 128 * 128 * 1024 * len(blocks),
            bytes_accessed=(2 + len(blocks)) << 20,
            transcendentals=0,
        ),
        name="triangle_products",
    )(*operands)


def per_device(pair, layernorm_gain, layernorm_bias, proj_weight, product_grad):
    rows, cols, width = pair.shape
    split = lambda x: jnp.transpose(x, (2, 1, 0)).reshape(GROUPS, width // GROUPS, cols, rows)
    gain = layernorm_gain.reshape(1, width)
    bias = layernorm_bias.reshape(1, width)
    slab = lax.axis_index("z").astype(jnp.int32).reshape(1)

    own = all_to_all(split(product_grad), PLANE)
    up1, down1 = shift(own, 1), shift(own, -1)
    pair, own = lax.optimization_barrier((pair, own))
    left, right = pre(pair, gain, bias, proj_weight)
    left = all_to_all(split(left), PLANE)
    right, left, up1, down1 = lax.optimization_barrier((split(right), left, up1, down1))
    up2, down2 = shift(up1, 1), shift(down1, -1)
    right = all_to_all(right, PLANE)
    up2, down2, right = lax.optimization_barrier((up2, down2, right))
    up3, down3 = shift(up2, 1), shift(down2, -1)
    sums = products(
        slab, left, right,
        [(0, [own]), (7, [up1]), (1, [down1]), (6, [up2]), (2, [down2])], None, False,
    )
    up4, down4 = shift(up3[:16], 1), shift(down3[16:], -1)
    sums = products(slab, left, right, [(5, [up3]), (3, [down3])], sums, False)
    back = products(slab, left, right, [(4, [up4, down4])], sums, True)
    back = all_to_all(back, PLANE)

    join = lambda x: jnp.transpose(x.reshape(width, cols, rows), (2, 1, 0))
    total_rows = 24 * GROUPS
    pairwise_gradient, total = post(
        pair, join(back[:, 0]), join(back[:, 1]), gain, bias, proj_weight, total_rows
    )
    total = jnp.sum(all_to_all(total.reshape(GROUPS, 24, width), PLANE), axis=0)
    total = lax.psum(total, "z") / (rows * 8)
    total = all_to_all(jnp.broadcast_to(total[None], (GROUPS, 24, width)), PLANE)
    total = total.reshape(total_rows, width)
    proj_grad = jnp.transpose(total[: 4 * width].reshape(4, width, width), (1, 0, 2))
    proj_grad = proj_grad.reshape(width, 4 * width)
    layernorm_gradient = jnp.stack([total[4 * width], total[4 * width + 8]])
    return pairwise_gradient, proj_grad, layernorm_gradient


def solution(mesh):
    fine = Mesh(mesh.devices.reshape(4, 2, 2, 8, 2), ("y", "xh", "xl", "z", "c"))
    tiles = P(("y", "xh"), ("xl", "z", "c"), None)
    return jax.shard_map(
        per_device,
        mesh=fine,
        in_specs=(tiles, P(), P(), P(), tiles),
        out_specs=(tiles, P(), P()),
        check_vma=False,
    )
```

```python
import functools

import jax
import jax.numpy as jnp
from jax import lax
from jax.experimental import pallas as pl
from jax.experimental.pallas import tpu as pltpu
from jax.sharding import Mesh, PartitionSpec as P

PLANE = ("y", "xh", "xl", "c")
GROUPS = 32
SLABS = 8
STEP_ROWS = 16
VMEM_LIMIT = 48 * 1024 * 1024


def all_to_all(x, axes):
    return lax.all_to_all(x, axes, split_axis=0, concat_axis=0, tiled=True)


def shift(x, by):
    return lax.ppermute(x, "z", [(i, (i + by) % SLABS) for i in range(SLABS)])


def normalize(pair_ref, gain_ref, bias_ref):
    x = pair_ref[...].astype(jnp.float32)
    x = x.reshape(x.shape[0] * x.shape[1], x.shape[2])
    centred = x - jnp.mean(x, axis=1, keepdims=True)
    inverse = lax.rsqrt(jnp.mean(centred * centred, axis=1, keepdims=True) + 1e-05)
    xhat = centred * inverse
    normed = (xhat * gain_ref[...] + bias_ref[...]).astype(jnp.bfloat16)
    return xhat, inverse, normed


def lane_order(transposed):
    source = lax.broadcasted_iota(jnp.int32, (128, 128), 1 if transposed else 0)
    lane = lax.broadcasted_iota(jnp.int32, (128, 128), 0 if transposed else 1)
    wanted = ((lane >> 1) & 1) * 64 + (lane >> 2) * 2 + (lane & 1)
    return jnp.where(source == wanted, 1.0, 0.0).astype(jnp.float32)


def pre_kernel(pair_ref, gain_ref, bias_ref, weight_ref, a_ref, b_ref, ordered_ref):
    @pl.when(pl.program_id(0) == 0)
    def _():
        order = lane_order(False).astype(jnp.bfloat16)
        for half in range(2):
            for kind in range(2):
                left = weight_ref[:, 128 * kind + 64 * half : 128 * kind + 64 * half + 64]
                right = weight_ref[:, 256 + 128 * kind + 64 * half : 320 + 128 * kind + 64 * half]
                at = 256 * half + 128 * kind
                ordered_ref[:, at : at + 128] = jnp.dot(
                    jnp.concatenate([left, right], axis=1),
                    order,
                    preferred_element_type=jnp.float32,
                ).astype(jnp.bfloat16)

    _, _, normed = normalize(pair_ref, gain_ref, bias_ref)
    proj = jnp.dot(normed, ordered_ref[...], preferred_element_type=jnp.float32)
    for half, ref in enumerate((a_ref, b_ref)):
        value = proj[:, 256 * half : 256 * half + 128]
        gate = proj[:, 256 * half + 128 : 256 * half + 256]
        ref[...] = (jax.nn.sigmoid(gate) * value).astype(jnp.bfloat16).reshape(ref.shape)


def pre(pair, gain, bias, weight):
    rows, cols, width = pair.shape
    tile = pl.BlockSpec((STEP_ROWS, cols, width), lambda i: (i, 0, 0))
    whole = lambda *shape: pl.BlockSpec(shape, lambda i: (0,) * len(shape))
    return pl.pallas_call(
        pre_kernel,
        grid=(rows // STEP_ROWS,),
        in_specs=[tile, whole(1, width), whole(1, width), whole(*weight.shape)],
        out_specs=[tile, tile, whole(*weight.shape)],
        out_shape=[jax.ShapeDtypeStruct(pair.shape, jnp.bfloat16)] * 2
        + [jax.ShapeDtypeStruct(weight.shape, jnp.bfloat16)],
        compiler_params=pltpu.CompilerParams(vmem_limit_bytes=VMEM_LIMIT),
        cost_estimate=pl.CostEstimate(
            flops=2 * rows * cols * width * 512, bytes_accessed=12 << 20, transcendentals=1 << 20
        ),
        name="gated_projections",
    )(pair, gain, bias, weight)


def post_kernel(
    pair_ref, a_ref, b_ref, gain_ref, bias_ref, ordered_ref, grad_ref, total_ref, wgrad_ref
):
    step = pl.program_id(0)

    @pl.when(step == 0)
    def _():
        total_ref[...] = jnp.zeros_like(total_ref)
        wgrad_ref[...] = jnp.zeros_like(wgrad_ref)

    xhat, inverse, normed = normalize(pair_ref, gain_ref, bias_ref)
    proj = jnp.dot(normed, ordered_ref[...], preferred_element_type=jnp.float32)
    width = xhat.shape[1]
    parts = []
    for half, ref in enumerate((a_ref, b_ref)):
        value = proj[:, 256 * half : 256 * half + 128]
        gate = jax.nn.sigmoid(proj[:, 256 * half + 128 : 256 * half + 256])
        gated = ref[...].astype(jnp.float32).reshape(xhat.shape) * gate
        parts.append(gated.astype(jnp.bfloat16))
        parts.append((gated * value * (1.0 - gate)).astype(jnp.bfloat16))
    dproj = jnp.concatenate(parts, axis=1)
    dnormed = lax.dot_general(
        dproj, ordered_ref[...], (((1,), (1,)), ((), ())), preferred_element_type=jnp.float32
    )
    wgrad_ref[...] += lax.dot_general(
        normed, dproj, (((0,), (0,)), ((), ())), preferred_element_type=jnp.float32
    )
    total_ref[4 * width : 4 * width + 1, :] += jnp.sum(dnormed * xhat, axis=0, keepdims=True)
    total_ref[4 * width + 8 : 4 * width + 9, :] += jnp.sum(dnormed, axis=0, keepdims=True)
    g = dnormed * gain_ref[...]
    grad = (
        g
        - jnp.mean(g, axis=1, keepdims=True)
        - xhat * jnp.mean(g * xhat, axis=1, keepdims=True)
    ) * inverse
    grad_ref[...] = grad.astype(jnp.bfloat16).reshape(grad_ref.shape)

    @pl.when(step == pl.num_programs(0) - 1)
    def _():
        order = lane_order(True)
        plain = [
            jnp.dot(
                wgrad_ref[:, 128 * n : 128 * n + 128],
                order,
                precision=lax.Precision.HIGHEST,
                preferred_element_type=jnp.float32,
            )
            for n in range(4)
        ]
        for side in range(2):
            for kind in range(2):
                at = (2 * side + kind) * width
                total_ref[at : at + width, :] = jnp.concatenate(
                    [plain[2 * half + kind][:, 64 * side : 64 * side + 64] for half in range(2)],
                    axis=1,
                )


def post(pair, a, b, gain, bias, ordered, total_rows):
    rows, cols, width = pair.shape
    tile = pl.BlockSpec((STEP_ROWS, cols, width), lambda i: (i, 0, 0))
    whole = lambda *shape: pl.BlockSpec(shape, lambda i: (0,) * len(shape))
    return pl.pallas_call(
        post_kernel,
        grid=(rows // STEP_ROWS,),
        in_specs=[tile, tile, tile, whole(1, width), whole(1, width), whole(*ordered.shape)],
        out_specs=[tile, whole(total_rows, width)],
        out_shape=[
            jax.ShapeDtypeStruct(pair.shape, jnp.bfloat16),
            jax.ShapeDtypeStruct((total_rows, width), jnp.float32),
        ],
        scratch_shapes=[pltpu.VMEM(ordered.shape, jnp.float32)],
        compiler_params=pltpu.CompilerParams(vmem_limit_bytes=VMEM_LIMIT),
        cost_estimate=pl.CostEstimate(
            flops=6 * rows * cols * width * 512, bytes_accessed=20 << 20, transcendentals=1 << 20
        ),
        name="input_gradients",
    )(pair, a, b, gain, bias, ordered)


def assemble(ref, at):
    return jnp.concatenate(
        [
            jnp.concatenate([ref[4 * r + c, at] for c in range(4)], axis=0)
            for r in range(8)
        ],
        axis=1,
    )


def product_kernel(offsets, slab_ref, sides_ref, *refs):
    block_refs = refs[: len(offsets)]
    out_ref, grads = refs[len(offsets) :]
    slab = slab_ref[0]
    for offset, ref in zip(offsets, block_refs):
        where = lax.rem(slab + offset, SLABS)
        for x in range(2):
            rows = pl.ds(pl.multiple_of(512 * x + 64 * where, 64), 64)
            for r in range(8):
                grads[rows, 128 * r : 128 * r + 128] = jnp.concatenate(
                    [ref[4 * r + 2 * x, 0], ref[4 * r + 2 * x + 1, 0]], axis=0
                )
    left = assemble(sides_ref.at[:, 0], 0)
    right = assemble(sides_ref.at[:, 1], 0)
    first = jnp.dot(right, grads[...], preferred_element_type=jnp.float32)
    second = lax.dot_general(
        left, grads[...], (((1,), (1,)), ((), ())), preferred_element_type=jnp.float32
    )
    for side, value in enumerate((first, second)):
        value = value.astype(jnp.bfloat16)
        for r in range(8):
            for c in range(4):
                out_ref[4 * r + c, side, 0] = value[
                    32 * c : 32 * c + 32, 128 * r : 128 * r + 128
                ]


def products(slab, sides, blocks):
    groups, pairs, depth, width = sides.shape
    channels = pairs // 2
    sides = sides.reshape(groups, 2, channels, depth, width)
    sides_spec = pl.BlockSpec((groups, 2, 1, depth, width), lambda h: (0, 0, h, 0, 0))
    piece = pl.BlockSpec((groups, 1, depth, width), lambda h: (0, h, 0, 0))
    out = pl.pallas_call(
        functools.partial(product_kernel, [offset for offset, _ in blocks]),
        grid=(channels,),
        in_specs=[pl.BlockSpec(memory_space=pltpu.SMEM), sides_spec] + [piece] * len(blocks),
        out_specs=sides_spec,
        out_shape=jax.ShapeDtypeStruct(sides.shape, jnp.bfloat16),
        scratch_shapes=[pltpu.VMEM((1024, 1024), jnp.bfloat16)],
        compiler_params=pltpu.CompilerParams(vmem_limit_bytes=VMEM_LIMIT),
        cost_estimate=pl.CostEstimate(
            flops=4 * channels * 128 * 1024 * 1024, bytes_accessed=12 << 20, transcendentals=0
        ),
        name="triangle_products",
    )(slab, sides, *[block for _, block in blocks])
    return out.reshape(groups, pairs, depth, width)


def per_device(pair, layernorm_gain, layernorm_bias, proj_weight, product_grad):
    rows, cols, width = pair.shape
    barrier = lax.optimization_barrier
    split = lambda x: jnp.transpose(x, (2, 1, 0)).reshape(GROUPS, -1, cols, rows)
    join = lambda x: jnp.transpose(x.reshape(width, cols, rows), (2, 1, 0))
    gain = layernorm_gain.reshape(1, width)
    bias = layernorm_bias.reshape(1, width)
    slab = lax.axis_index("z").astype(jnp.int32).reshape(1)
    both = lambda pair_of: (shift(pair_of[0], 1), shift(pair_of[1], -1))

    half = width // 2
    a0 = all_to_all(split(product_grad[:, :, :half]), PLANE)
    a1 = both((a0, a0))
    sides_a, sides_b, ordered = pre(pair, gain, bias, proj_weight)
    b0, a0 = barrier((split(product_grad[:, :, half:]), a0))
    b0 = all_to_all(b0, PLANE)
    sides_a, b0, a1 = barrier((split(sides_a), b0, a1))
    a2 = both(a1)
    b1 = both((b0, b0))
    sides_a = all_to_all(sides_a, PLANE)
    sides_b, sides_a, a2, b1 = barrier((split(sides_b), sides_a, a2, b1))
    a3 = both(a2)
    b2 = both(b1)
    sides_b = all_to_all(sides_b, PLANE)
    sides_b, a3, b2 = barrier((sides_b, a3, b2))
    a4 = shift(a3[0], 1)
    b3 = both(b2)
    near = lambda x0, x1, x2, x3: [
        (0, x0), (7, x1[0]), (1, x1[1]), (6, x2[0]), (2, x2[1]), (5, x3[0]), (3, x3[1])
    ]
    back_a = products(slab, sides_a, near(a0, a1, a2, a3) + [(4, a4)])
    b4 = shift(b3[1], -1)
    back_a = all_to_all(back_a, PLANE)
    back_b = products(slab, sides_b, near(b0, b1, b2, b3) + [(4, b4)])
    back_b = all_to_all(back_b, PLANE)

    total_rows = 24 * GROUPS
    pairwise_gradient, total = post(
        pair, join(back_a), join(back_b), gain, bias, ordered, total_rows
    )
    total = jnp.sum(all_to_all(total.reshape(GROUPS, 24, width), PLANE), axis=0)
    total = all_to_all(jnp.broadcast_to(total[None], (SLABS, 24, width)), "z")
    total = jnp.sum(total, axis=0) / (rows * 8)
    total = all_to_all(jnp.broadcast_to(total[None], (GROUPS, 24, width)), PLANE)
    total = total.reshape(total_rows, width)
    proj_grad = jnp.transpose(total[: 4 * width].reshape(4, width, width), (1, 0, 2))
    proj_grad = proj_grad.reshape(width, 4 * width)
    layernorm_gradient = jnp.stack([total[4 * width], total[4 * width + 8]])
    return pairwise_gradient, proj_grad, layernorm_gradient


def solution(mesh):
    fine = Mesh(mesh.devices.reshape(4, 2, 2, 8, 2), ("y", "xh", "xl", "z", "c"))
    tiles = P(("y", "xh"), ("xl", "z", "c"), None)
    return jax.shard_map(
        per_device,
        mesh=fine,
        in_specs=(tiles, P(), P(), P(), tiles),
        out_specs=(tiles, P(), P()),
        check_vma=False,
    )
```

```python
import functools

import jax
import jax.numpy as jnp
from jax import lax
from jax.experimental import pallas as pl
from jax.experimental.pallas import tpu as pltpu
from jax.sharding import Mesh, PartitionSpec as P

PLANE = ("y", "xh", "xl", "c")
GROUPS = 32
SLABS = 8
STEP_ROWS = 64
VMEM_LIMIT = 48 * 1024 * 1024


def all_to_all(x, axes):
    return lax.all_to_all(x, axes, split_axis=0, concat_axis=0, tiled=True)


def shift(x, by):
    return lax.ppermute(x, "z", [(i, (i + by) % SLABS) for i in range(SLABS)])


def normalize(pair_ref, gain_ref, bias_ref):
    x = pair_ref[...].astype(jnp.float32)
    x = x.reshape(x.shape[0] * x.shape[1], x.shape[2])
    centred = x - jnp.mean(x, axis=1, keepdims=True)
    inverse = lax.rsqrt(jnp.mean(centred * centred, axis=1, keepdims=True) + 1e-05)
    xhat = centred * inverse
    normed = (xhat * gain_ref[...] + bias_ref[...]).astype(jnp.bfloat16)
    return xhat, inverse, normed


def lane_order(transposed):
    source = lax.broadcasted_iota(jnp.int32, (128, 128), 1 if transposed else 0)
    lane = lax.broadcasted_iota(jnp.int32, (128, 128), 0 if transposed else 1)
    wanted = ((lane >> 1) & 1) * 64 + (lane >> 2) * 2 + (lane & 1)
    return jnp.where(source == wanted, 1.0, 0.0).astype(jnp.float32)


def pre_kernel(pair_ref, gain_ref, bias_ref, weight_ref, a_ref, b_ref, ordered_ref):
    @pl.when(pl.program_id(0) == 0)
    def _():
        order = lane_order(False).astype(jnp.bfloat16)
        for half in range(2):
            for kind in range(2):
                left = weight_ref[:, 128 * kind + 64 * half : 128 * kind + 64 * half + 64]
                right = weight_ref[:, 256 + 128 * kind + 64 * half : 320 + 128 * kind + 64 * half]
                at = 256 * half + 128 * kind
                ordered_ref[:, at : at + 128] = jnp.dot(
                    jnp.concatenate([left, right], axis=1),
                    order,
                    preferred_element_type=jnp.float32,
                ).astype(jnp.bfloat16)

    _, _, normed = normalize(pair_ref, gain_ref, bias_ref)
    proj = jnp.dot(normed, ordered_ref[...], preferred_element_type=jnp.float32)
    for half, ref in enumerate((a_ref, b_ref)):
        value = proj[:, 256 * half : 256 * half + 128]
        gate = proj[:, 256 * half + 128 : 256 * half + 256]
        ref[...] = (jax.nn.sigmoid(gate) * value).astype(jnp.bfloat16).reshape(ref.shape)


def pre(pair, gain, bias, weight):
    rows, cols, width = pair.shape
    tile = pl.BlockSpec((STEP_ROWS, cols, width), lambda i: (i, 0, 0))
    whole = lambda *shape: pl.BlockSpec(shape, lambda i: (0,) * len(shape))
    return pl.pallas_call(
        pre_kernel,
        grid=(rows // STEP_ROWS,),
        in_specs=[tile, whole(1, width), whole(1, width), whole(*weight.shape)],
        out_specs=[tile, tile, whole(*weight.shape)],
        out_shape=[jax.ShapeDtypeStruct(pair.shape, jnp.bfloat16)] * 2
        + [jax.ShapeDtypeStruct(weight.shape, jnp.bfloat16)],
        compiler_params=pltpu.CompilerParams(vmem_limit_bytes=VMEM_LIMIT),
        cost_estimate=pl.CostEstimate(
            flops=2 * rows * cols * width * 512, bytes_accessed=12 << 20, transcendentals=1 << 20
        ),
        name="gated_projections",
    )(pair, gain, bias, weight)


def post_kernel(
    pair_ref, a_ref, b_ref, gain_ref, bias_ref, ordered_ref, grad_ref, total_ref, wgrad_ref
):
    step = pl.program_id(0)

    @pl.when(step == 0)
    def _():
        total_ref[...] = jnp.zeros_like(total_ref)
        wgrad_ref[...] = jnp.zeros_like(wgrad_ref)

    xhat, inverse, normed = normalize(pair_ref, gain_ref, bias_ref)
    proj = jnp.dot(normed, ordered_ref[...], preferred_element_type=jnp.float32)
    width = xhat.shape[1]
    parts = []
    for half, ref in enumerate((a_ref, b_ref)):
        value = proj[:, 256 * half : 256 * half + 128]
        gate = jax.nn.sigmoid(proj[:, 256 * half + 128 : 256 * half + 256])
        gated = ref[...].astype(jnp.float32).reshape(xhat.shape) * gate
        parts.append(gated.astype(jnp.bfloat16))
        parts.append((gated * value * (1.0 - gate)).astype(jnp.bfloat16))
    dproj = jnp.concatenate(parts, axis=1)
    dnormed = lax.dot_general(
        dproj, ordered_ref[...], (((1,), (1,)), ((), ())), preferred_element_type=jnp.float32
    )
    wgrad_ref[...] += lax.dot_general(
        normed, dproj, (((0,), (0,)), ((), ())), preferred_element_type=jnp.float32
    )
    total_ref[4 * width : 4 * width + 1, :] += jnp.sum(dnormed * xhat, axis=0, keepdims=True)
    total_ref[4 * width + 8 : 4 * width + 9, :] += jnp.sum(dnormed, axis=0, keepdims=True)
    g = dnormed * gain_ref[...]
    grad = (
        g
        - jnp.mean(g, axis=1, keepdims=True)
        - xhat * jnp.mean(g * xhat, axis=1, keepdims=True)
    ) * inverse
    grad_ref[...] = grad.astype(jnp.bfloat16).reshape(grad_ref.shape)

    @pl.when(step == pl.num_programs(0) - 1)
    def _():
        order = lane_order(True)
        plain = [
            jnp.dot(
                wgrad_ref[:, 128 * n : 128 * n + 128],
                order,
                precision=lax.Precision.HIGHEST,
                preferred_element_type=jnp.float32,
            )
            for n in range(4)
        ]
        for side in range(2):
            for kind in range(2):
                at = (2 * side + kind) * width
                total_ref[at : at + width, :] = jnp.concatenate(
                    [plain[2 * half + kind][:, 64 * side : 64 * side + 64] for half in range(2)],
                    axis=1,
                )


def post(pair, a, b, gain, bias, ordered, total_rows):
    rows, cols, width = pair.shape
    tile = pl.BlockSpec((STEP_ROWS, cols, width), lambda i: (i, 0, 0))
    whole = lambda *shape: pl.BlockSpec(shape, lambda i: (0,) * len(shape))
    return pl.pallas_call(
        post_kernel,
        grid=(rows // STEP_ROWS,),
        in_specs=[tile, tile, tile, whole(1, width), whole(1, width), whole(*ordered.shape)],
        out_specs=[tile, whole(total_rows, width)],
        out_shape=[
            jax.ShapeDtypeStruct(pair.shape, jnp.bfloat16),
            jax.ShapeDtypeStruct((total_rows, width), jnp.float32),
        ],
        scratch_shapes=[pltpu.VMEM(ordered.shape, jnp.float32)],
        compiler_params=pltpu.CompilerParams(vmem_limit_bytes=VMEM_LIMIT),
        cost_estimate=pl.CostEstimate(
            flops=6 * rows * cols * width * 512, bytes_accessed=20 << 20, transcendentals=1 << 20
        ),
        name="input_gradients",
    )(pair, a, b, gain, bias, ordered)


def assemble(ref, at):
    return jnp.concatenate(
        [
            jnp.concatenate([ref[4 * r + c, at] for c in range(4)], axis=0)
            for r in range(8)
        ],
        axis=1,
    )


def product_kernel(offsets, slab_ref, sides_ref, *refs):
    block_refs, out_ref, grads = refs[:-2], refs[-2], refs[-1]
    if offsets is None:
        blocks = [(z, block_refs[0].at[z]) for z in range(SLABS)]
    else:
        blocks = [
            (lax.rem(slab_ref[0] + offset, SLABS), ref) for offset, ref in zip(offsets, block_refs)
        ]
    def place(where, ref):
        for x in range(2):
            rows = pl.ds(pl.multiple_of(512 * x + 64 * where, 64), 64)
            for r in range(8):
                grads[rows, 128 * r : 128 * r + 128] = jnp.concatenate(
                    [ref[4 * r + 2 * x, 0], ref[4 * r + 2 * x + 1, 0]], axis=0
                )

    for where, ref in blocks:
        place(where, ref)
    if offsets is not None:
        for channel in range(2):
            pl.when(pl.program_id(0) == channel)(
                functools.partial(
                    place, lax.rem(slab_ref[0] + 4, SLABS), block_refs[len(offsets) + channel]
                )
            )
    left = assemble(sides_ref.at[:, 0], 0)
    right = assemble(sides_ref.at[:, 1], 0)
    first = jnp.dot(right, grads[...], preferred_element_type=jnp.float32)
    second = lax.dot_general(
        left, grads[...], (((1,), (1,)), ((), ())), preferred_element_type=jnp.float32
    )
    for side, value in enumerate((first, second)):
        value = value.astype(jnp.bfloat16)
        for r in range(8):
            for c in range(4):
                out_ref[4 * r + c, side, 0] = value[
                    32 * c : 32 * c + 32, 128 * r : 128 * r + 128
                ]


def products(slab, sides, offsets, blocks):
    groups, pairs, depth, width = sides.shape
    channels = pairs // 2
    sides = sides.reshape(groups, 2, channels, depth, width)
    sides_spec = pl.BlockSpec((groups, 2, 1, depth, width), lambda h: (0, 0, h, 0, 0))
    if offsets is None:
        piece = pl.BlockSpec((SLABS, groups, 1, depth, width), lambda h: (0, 0, h, 0, 0))
    else:
        piece = pl.BlockSpec((groups, 1, depth, width), lambda h: (0, h, 0, 0))
    alone = pl.BlockSpec((groups, 1, depth, width), lambda h: (0, 0, 0, 0))
    pieces = [piece if block.shape[-3] == channels else alone for block in blocks]
    out = pl.pallas_call(
        functools.partial(product_kernel, offsets),
        grid=(channels,),
        in_specs=[pl.BlockSpec(memory_space=pltpu.SMEM), sides_spec] + pieces,
        out_specs=sides_spec,
        out_shape=jax.ShapeDtypeStruct(sides.shape, jnp.bfloat16),
        scratch_shapes=[pltpu.VMEM((1024, 1024), jnp.bfloat16)],
        compiler_params=pltpu.CompilerParams(vmem_limit_bytes=VMEM_LIMIT),
        cost_estimate=pl.CostEstimate(
            flops=4 * channels * 128 * 1024 * 1024, bytes_accessed=12 << 20, transcendentals=0
        ),
        name="triangle_products",
    )(slab, sides, *blocks)
    return out.reshape(groups, pairs, depth, width)


def per_device(pair, layernorm_gain, layernorm_bias, proj_weight, product_grad):
    rows, cols, width = pair.shape
    barrier = lax.optimization_barrier
    split = lambda x: jnp.transpose(x, (2, 1, 0)).reshape(GROUPS, -1, cols, rows)
    join = lambda x: jnp.transpose(x.reshape(width, cols, rows), (2, 1, 0))
    gain = layernorm_gain.reshape(1, width)
    bias = layernorm_bias.reshape(1, width)
    slab = lax.axis_index("z").astype(jnp.int32).reshape(1)
    both = lambda pair_of: (shift(pair_of[0], 1), shift(pair_of[1], -1))

    half = width // 2
    own_a = all_to_all(split(product_grad[:, :, :half]), PLANE)
    grads_a = lax.all_gather(own_a, "z", axis=0, tiled=False)
    sides_a, sides_b, ordered = pre(pair, gain, bias, proj_weight)
    own_b, own_a = barrier((split(product_grad[:, :, half:]), own_a))
    own_b = all_to_all(own_b, PLANE)
    b1 = both((own_b, own_b))
    sides_a, own_b = barrier((split(sides_a), own_b))
    sides_a = all_to_all(sides_a, PLANE)
    sides_b, sides_a, b1 = barrier((split(sides_b), sides_a, b1))
    b2 = both(b1)
    sides_b = all_to_all(sides_b, PLANE)
    sides_b, b2 = barrier((sides_b, b2))
    b3 = both(b2)
    sides_a, b3 = barrier((sides_a, b3))
    back_a = products(slab, sides_a, None, [grads_a])
    sides_b, back_a = barrier((sides_b, back_a))
    back_a = all_to_all(back_a, PLANE)
    b4 = shift(b3[0][:, :1], 1), shift(b3[1][:, 1:], -1)
    back_b = products(
        slab, sides_b, [0, 7, 1, 6, 2, 5, 3], [own_b, *b1, *b2, *b3, *b4]
    )
    back_b = all_to_all(back_b, PLANE)

    total_rows = 24 * GROUPS
    pairwise_gradient, total = post(
        pair, join(back_a), join(back_b), gain, bias, ordered, total_rows
    )
    total = jnp.sum(all_to_all(total.reshape(GROUPS, 24, width), PLANE), axis=0)
    total = all_to_all(jnp.broadcast_to(total[None], (SLABS, 24, width)), "z")
    total = jnp.sum(total, axis=0) / (rows * 8)
    total = all_to_all(jnp.broadcast_to(total[None], (GROUPS, 24, width)), PLANE)
    total = total.reshape(total_rows, width)
    proj_grad = jnp.transpose(total[: 4 * width].reshape(4, width, width), (1, 0, 2))
    proj_grad = proj_grad.reshape(width, 4 * width)
    layernorm_gradient = jnp.stack([total[4 * width], total[4 * width + 8]])
    return pairwise_gradient, proj_grad, layernorm_gradient


def solution(mesh):
    fine = Mesh(mesh.devices.reshape(4, 2, 2, 8, 2), ("y", "xh", "xl", "z", "c"))
    tiles = P(("y", "xh"), ("xl", "z", "c"), None)
    return jax.shard_map(
        per_device,
        mesh=fine,
        in_specs=(tiles, P(), P(), P(), tiles),
        out_specs=(tiles, P(), P()),
        check_vma=False,
    )
```

```python
import functools

import jax
import jax.numpy as jnp
from jax import lax
from jax.experimental import pallas as pl
from jax.experimental.pallas import tpu as pltpu
from jax.sharding import Mesh, PartitionSpec as P

PLANE = ("y", "xh", "xl", "c")
CHIPS = ("y", "xh", "xl")
GROUPS = 32
SLABS = 8
STEP_ROWS = 64
VMEM_LIMIT = 32 * 1024 * 1024


def all_to_all(x, axes):
    return lax.all_to_all(x, axes, split_axis=0, concat_axis=0, tiled=True)


def shift(x, by):
    return lax.ppermute(x, "z", [(i, (i + by) % SLABS) for i in range(SLABS)])


def normalize(pair_ref, gain_ref, bias_ref):
    x = pair_ref[...].astype(jnp.float32)
    x = x.reshape(x.shape[0] * x.shape[1], x.shape[2])
    centred = x - jnp.mean(x, axis=1, keepdims=True)
    inverse = lax.rsqrt(jnp.mean(centred * centred, axis=1, keepdims=True) + 1e-05)
    xhat = centred * inverse
    normed = (xhat * gain_ref[...] + bias_ref[...]).astype(jnp.bfloat16)
    return xhat, inverse, normed


def lane_order(transposed):
    source = lax.broadcasted_iota(jnp.int32, (256, 256), 1 if transposed else 0)
    lane = lax.broadcasted_iota(jnp.int32, (256, 256), 0 if transposed else 1)
    side, half = (lane >> 1) & 1, (lane >> 2) & 1
    wanted = side * 128 + (lane >> 3) * 4 + half * 2 + (lane & 1)
    return jnp.where(source == wanted, 1.0, 0.0).astype(jnp.float32)


def pre_kernel(pair_ref, gain_ref, bias_ref, weight_ref, sides_ref, ordered_ref):
    @pl.when(pl.program_id(0) == 0)
    def _():
        order = lane_order(False).astype(jnp.bfloat16)
        for kind in range(2):
            plain = jnp.concatenate(
                [weight_ref[:, at : at + 128] for at in (128 * kind, 256 + 128 * kind)], axis=1
            )
            ordered_ref[:, 256 * kind : 256 * kind + 256] = jnp.dot(
                plain, order, preferred_element_type=jnp.float32
            ).astype(jnp.bfloat16)

    _, _, normed = normalize(pair_ref, gain_ref, bias_ref)
    proj = jnp.dot(normed, ordered_ref[...], preferred_element_type=jnp.float32)
    sides = jax.nn.sigmoid(proj[:, 256:]) * proj[:, :256]
    sides_ref[...] = sides.astype(jnp.bfloat16).reshape(sides_ref.shape)


def pre(pair, gain, bias, weight):
    rows, cols, width = pair.shape
    tile = pl.BlockSpec((STEP_ROWS, cols, width), lambda i: (i, 0, 0))
    whole = lambda *shape: pl.BlockSpec(shape, lambda i: (0,) * len(shape))
    return pl.pallas_call(
        pre_kernel,
        grid=(rows // STEP_ROWS,),
        in_specs=[tile, whole(1, width), whole(1, width), whole(*weight.shape)],
        out_specs=[
            pl.BlockSpec((STEP_ROWS, cols, 2 * width), lambda i: (i, 0, 0)),
            whole(*weight.shape),
        ],
        out_shape=[
            jax.ShapeDtypeStruct((rows, cols, 2 * width), jnp.bfloat16),
            jax.ShapeDtypeStruct(weight.shape, jnp.bfloat16),
        ],
        compiler_params=pltpu.CompilerParams(vmem_limit_bytes=VMEM_LIMIT),
        cost_estimate=pl.CostEstimate(
            flops=2 * rows * cols * width * 512, bytes_accessed=12 << 20, transcendentals=1 << 20
        ),
        name="gated_projections",
    )(pair, gain, bias, weight)


def post_kernel(
    pair_ref, back_ref, gain_ref, bias_ref, ordered_ref, grad_ref, total_ref, wgrad_ref
):
    step = pl.program_id(0)

    @pl.when(step == 0)
    def _():
        total_ref[...] = jnp.zeros_like(total_ref)
        wgrad_ref[...] = jnp.zeros_like(wgrad_ref)

    xhat, inverse, normed = normalize(pair_ref, gain_ref, bias_ref)
    proj = jnp.dot(normed, ordered_ref[...], preferred_element_type=jnp.float32)
    width = xhat.shape[1]
    value, gate = proj[:, :256], jax.nn.sigmoid(proj[:, 256:])
    gated = back_ref[...].astype(jnp.float32).reshape(gate.shape) * gate
    dproj = jnp.concatenate(
        [gated.astype(jnp.bfloat16), (gated * value * (1.0 - gate)).astype(jnp.bfloat16)], axis=1
    )
    dnormed = lax.dot_general(
        dproj, ordered_ref[...], (((1,), (1,)), ((), ())), preferred_element_type=jnp.float32
    )
    wgrad_ref[...] += lax.dot_general(
        normed, dproj, (((0,), (0,)), ((), ())), preferred_element_type=jnp.float32
    )
    total_ref[4 * width : 4 * width + 1, :] += jnp.sum(dnormed * xhat, axis=0, keepdims=True)
    total_ref[4 * width + 8 : 4 * width + 9, :] += jnp.sum(dnormed, axis=0, keepdims=True)
    g = dnormed * gain_ref[...]
    grad = (
        g
        - jnp.mean(g, axis=1, keepdims=True)
        - xhat * jnp.mean(g * xhat, axis=1, keepdims=True)
    ) * inverse
    grad_ref[...] = grad.astype(jnp.bfloat16).reshape(grad_ref.shape)

    @pl.when(step == pl.num_programs(0) - 1)
    def _():
        order = lane_order(True)
        for kind in range(2):
            plain = jnp.dot(
                wgrad_ref[:, 256 * kind : 256 * kind + 256],
                order,
                precision=lax.Precision.HIGHEST,
                preferred_element_type=jnp.float32,
            )
            for side in range(2):
                at = (2 * side + kind) * width
                total_ref[at : at + width, :] = plain[:, 128 * side : 128 * side + 128]


def post(pair, back, gain, bias, ordered, total_rows):
    rows, cols, width = pair.shape
    tile = pl.BlockSpec((STEP_ROWS, cols, width), lambda i: (i, 0, 0))
    whole = lambda *shape: pl.BlockSpec(shape, lambda i: (0,) * len(shape))
    return pl.pallas_call(
        post_kernel,
        grid=(rows // STEP_ROWS,),
        in_specs=[
            tile,
            pl.BlockSpec((STEP_ROWS, cols, 2 * width), lambda i: (i, 0, 0)),
            whole(1, width),
            whole(1, width),
            whole(*ordered.shape),
        ],
        out_specs=[tile, whole(total_rows, width)],
        out_shape=[
            jax.ShapeDtypeStruct(pair.shape, jnp.bfloat16),
            jax.ShapeDtypeStruct((total_rows, width), jnp.float32),
        ],
        scratch_shapes=[pltpu.VMEM(ordered.shape, jnp.float32)],
        compiler_params=pltpu.CompilerParams(vmem_limit_bytes=VMEM_LIMIT),
        cost_estimate=pl.CostEstimate(
            flops=6 * rows * cols * width * 512, bytes_accessed=20 << 20, transcendentals=1 << 20
        ),
        name="input_gradients",
    )(pair, back, gain, bias, ordered)


def assemble(ref, at):
    return jnp.concatenate(
        [
            jnp.concatenate([ref[4 * r + c, at] for c in range(4)], axis=0)
            for r in range(8)
        ],
        axis=1,
    )


def product_kernel(second_half, slab_ref, sides_ref, *refs):
    *block_refs, up_ref, down_ref = refs[: 9]
    out_ref, grads = refs[9 + second_half :]

    def place(offset, ref):
        where = lax.rem(slab_ref[0] + offset, SLABS)
        for x in range(2):
            rows = pl.ds(pl.multiple_of(512 * x + 64 * where, 64), 64)
            for r in range(8):
                grads[rows, 128 * r : 128 * r + 128] = jnp.concatenate(
                    [ref[4 * r + 2 * x, 0], ref[4 * r + 2 * x + 1, 0]], axis=0
                )

    for offset, ref in zip((0, 7, 1, 6, 2, 5, 3), block_refs):
        place(offset, ref)
    for channel, ref in enumerate((up_ref, down_ref)):
        pl.when(pl.program_id(0) == channel)(functools.partial(place, 4, ref))
    left = assemble(sides_ref.at[:, 0], 0)
    right = assemble(sides_ref.at[:, 1], 0)
    first = jnp.dot(right, grads[...], preferred_element_type=jnp.float32)
    second = lax.dot_general(
        left, grads[...], (((1,), (1,)), ((), ())), preferred_element_type=jnp.float32
    )
    for side, value in enumerate((first, second)):
        value = value.astype(jnp.bfloat16)
        for r in range(8):
            for c in range(4):
                out_ref[4 * r + c, side, 0] = value[
                    32 * c : 32 * c + 32, 128 * r : 128 * r + 128
                ]


def products(slab, sides, half, blocks, earlier=None):
    groups, pairs, depth, width = sides.shape
    channels = pairs // 4
    sides = sides.reshape(groups, 4, channels, depth, width)
    sides_spec = pl.BlockSpec((groups, 2, 1, depth, width), lambda h: (0, half, h, 0, 0))
    piece = pl.BlockSpec((groups, 1, depth, width), lambda h: (0, h, 0, 0))
    alone = pl.BlockSpec((groups, 1, depth, width), lambda h: (0, 0, 0, 0))
    operands = [slab, sides, *blocks]
    specs = [pl.BlockSpec(memory_space=pltpu.SMEM), sides_spec] + [piece] * 7 + [alone] * 2
    if earlier is not None:
        operands.append(earlier)
        specs.append(pl.BlockSpec(memory_space=pl.ANY))
    return pl.pallas_call(
        functools.partial(product_kernel, earlier is not None),
        grid=(channels,),
        in_specs=specs,
        out_specs=sides_spec,
        out_shape=jax.ShapeDtypeStruct(sides.shape, jnp.bfloat16),
        scratch_shapes=[pltpu.VMEM((1024, 1024), jnp.bfloat16)],
        input_output_aliases={} if earlier is None else {len(operands) - 1: 0},
        compiler_params=pltpu.CompilerParams(vmem_limit_bytes=VMEM_LIMIT),
        cost_estimate=pl.CostEstimate(
            flops=4 * channels * 128 * 1024 * 1024, bytes_accessed=12 << 20, transcendentals=0
        ),
        name="triangle_products",
    )(*operands)


def sum_of_all(x):
    me = lax.axis_index("c")
    swap = lambda x: lax.ppermute(x, "c", [(0, 1), (1, 0)])
    mine = lax.dynamic_index_in_dim(x, me, 0, keepdims=False)
    others = lax.dynamic_index_in_dim(x, 1 - me, 0, keepdims=False)
    part = jnp.sum(all_to_all(mine + swap(others), CHIPS), axis=0)
    part = jnp.sum(all_to_all(jnp.broadcast_to(part, (SLABS,) + part.shape), "z"), axis=0)
    mine = all_to_all(jnp.broadcast_to(part, x.shape[1:]), CHIPS)
    others = swap(mine)
    first = me == 0
    return jnp.stack([jnp.where(first, mine, others), jnp.where(first, others, mine)])


def per_device(pair, layernorm_gain, layernorm_bias, proj_weight, product_grad):
    rows, cols, width = pair.shape
    barrier = lax.optimization_barrier
    split = lambda x: jnp.transpose(x, (2, 1, 0)).reshape(GROUPS, -1, cols, rows)
    join = lambda x: jnp.transpose(x.reshape(-1, cols, rows), (2, 1, 0))
    gain = layernorm_gain.reshape(1, width)
    bias = layernorm_bias.reshape(1, width)
    slab = lax.axis_index("z").astype(jnp.int32).reshape(1)
    both = lambda pair_of: (shift(pair_of[0], 1), shift(pair_of[1], -1))

    after = lambda wanted, done: barrier((wanted, done))[0]
    own = all_to_all(split(product_grad), PLANE)
    sides, ordered = pre(pair, gain, bias, proj_weight)
    own, sides = barrier((own, split(sides)))
    sides = all_to_all(sides, PLANE)
    a0, b0 = barrier((own[:, :2], own[:, 2:]))
    a1 = both((a0, a0))
    b1 = both((b0, b0))
    a1 = barrier(a1)
    a2 = both(a1)
    b1 = after(b1, a1)
    b2 = both(b1)
    a2 = after(a2, b1)
    a3 = both(a2)
    b2 = after(b2, a2)
    b3 = both(b2)
    a3 = after(a3, b2)
    a4 = shift(a3[0][:, :1], 1), shift(a3[1][:, 1:], -1)
    b3 = after(b3, a3)
    b4 = shift(b3[0][:, :1], 1), shift(b3[1][:, 1:], -1)
    back = products(slab, sides, 0, [a0, *a1, *a2, *a3, *a4])
    back = products(slab, sides, 1, [b0, *b1, *b2, *b3, *b4], back)
    back = all_to_all(back.reshape(sides.shape), PLANE)

    total_rows = 24 * GROUPS
    pairwise_gradient, total = post(
        pair, join(back), gain, bias, ordered, total_rows
    )
    total = sum_of_all(total.reshape(2, 16, 24, width)) / (rows * 8)
    total = total.reshape(total_rows, width)
    proj_grad = jnp.transpose(total[: 4 * width].reshape(4, width, width), (1, 0, 2))
    proj_grad = proj_grad.reshape(width, 4 * width)
    layernorm_gradient = jnp.stack([total[4 * width], total[4 * width + 8]])
    return pairwise_gradient, proj_grad, layernorm_gradient


def solution(mesh):
    fine = Mesh(mesh.devices.reshape(4, 2, 2, 8, 2), ("y", "xh", "xl", "z", "c"))
    tiles = P(("y", "xh"), ("xl", "z", "c"), None)
    return jax.shard_map(
        per_device,
        mesh=fine,
        in_specs=(tiles, P(), P(), P(), tiles),
        out_specs=(tiles, P(), P()),
        check_vma=False,
    )
```

```python
import functools

import jax
import jax.numpy as jnp
from jax import lax
from jax.experimental import pallas as pl
from jax.experimental.pallas import tpu as pltpu
from jax.sharding import Mesh, PartitionSpec as P

PLANE = ("y", "xh", "xl", "c")
CHIPS = ("y", "xh", "xl")
GROUPS = 32
SLABS = 8
STEP_ROWS = 64
VMEM_LIMIT = 32 * 1024 * 1024
PRODUCT_LIMIT = 58 * 1024 * 1024


def all_to_all(x, axes):
    return lax.all_to_all(x, axes, split_axis=0, concat_axis=0, tiled=True)


def shift(x, by):
    return lax.ppermute(x, "z", [(i, (i + by) % SLABS) for i in range(SLABS)])


def normalize(pair_ref, gain_ref, bias_ref):
    x = pair_ref[...].astype(jnp.float32)
    x = x.reshape(x.shape[0] * x.shape[1], x.shape[2])
    centred = x - jnp.mean(x, axis=1, keepdims=True)
    inverse = lax.rsqrt(jnp.mean(centred * centred, axis=1, keepdims=True) + 1e-05)
    xhat = centred * inverse
    normed = (xhat * gain_ref[...] + bias_ref[...]).astype(jnp.bfloat16)
    return xhat, inverse, normed


def lane_order(transposed):
    source = lax.broadcasted_iota(jnp.int32, (256, 256), 1 if transposed else 0)
    lane = lax.broadcasted_iota(jnp.int32, (256, 256), 0 if transposed else 1)
    side, half = (lane >> 1) & 1, (lane >> 2) & 1
    wanted = side * 128 + (lane >> 3) * 4 + half * 2 + (lane & 1)
    return jnp.where(source == wanted, 1.0, 0.0).astype(jnp.float32)


def pre_kernel(pair_ref, gain_ref, bias_ref, weight_ref, sides_ref, ordered_ref):
    @pl.when(pl.program_id(0) == 0)
    def _():
        order = lane_order(False).astype(jnp.bfloat16)
        for kind in range(2):
            plain = jnp.concatenate(
                [weight_ref[:, at : at + 128] for at in (128 * kind, 256 + 128 * kind)], axis=1
            )
            ordered_ref[:, 256 * kind : 256 * kind + 256] = jnp.dot(
                plain, order, preferred_element_type=jnp.float32
            ).astype(jnp.bfloat16)

    _, _, normed = normalize(pair_ref, gain_ref, bias_ref)
    proj = jnp.dot(normed, ordered_ref[...], preferred_element_type=jnp.float32)
    sides = jax.nn.sigmoid(proj[:, 256:]) * proj[:, :256]
    sides_ref[...] = sides.astype(jnp.bfloat16).reshape(sides_ref.shape)


def pre(pair, gain, bias, weight):
    rows, cols, width = pair.shape
    tile = pl.BlockSpec((STEP_ROWS, cols, width), lambda i: (i, 0, 0))
    whole = lambda *shape: pl.BlockSpec(shape, lambda i: (0,) * len(shape))
    return pl.pallas_call(
        pre_kernel,
        grid=(rows // STEP_ROWS,),
        in_specs=[tile, whole(1, width), whole(1, width), whole(*weight.shape)],
        out_specs=[
            pl.BlockSpec((STEP_ROWS, cols, 2 * width), lambda i: (i, 0, 0)),
            whole(*weight.shape),
        ],
        out_shape=[
            jax.ShapeDtypeStruct((rows, cols, 2 * width), jnp.bfloat16),
            jax.ShapeDtypeStruct(weight.shape, jnp.bfloat16),
        ],
        compiler_params=pltpu.CompilerParams(vmem_limit_bytes=VMEM_LIMIT),
        cost_estimate=pl.CostEstimate(
            flops=2 * rows * cols * width * 512, bytes_accessed=12 << 20, transcendentals=1 << 20
        ),
        name="gated_projections",
    )(pair, gain, bias, weight)


def post_kernel(
    pair_ref, back_ref, gain_ref, bias_ref, ordered_ref, grad_ref, total_ref, wgrad_ref
):
    step = pl.program_id(0)

    @pl.when(step == 0)
    def _():
        total_ref[...] = jnp.zeros_like(total_ref)
        wgrad_ref[...] = jnp.zeros_like(wgrad_ref)

    xhat, inverse, normed = normalize(pair_ref, gain_ref, bias_ref)
    proj = jnp.dot(normed, ordered_ref[...], preferred_element_type=jnp.float32)
    width = xhat.shape[1]
    value, gate = proj[:, :256], jax.nn.sigmoid(proj[:, 256:])
    gated = back_ref[...].astype(jnp.float32).reshape(gate.shape) * gate
    dproj = jnp.concatenate(
        [gated.astype(jnp.bfloat16), (gated * value * (1.0 - gate)).astype(jnp.bfloat16)], axis=1
    )
    dnormed = lax.dot_general(
        dproj, ordered_ref[...], (((1,), (1,)), ((), ())), preferred_element_type=jnp.float32
    )
    wgrad_ref[...] += lax.dot_general(
        normed, dproj, (((0,), (0,)), ((), ())), preferred_element_type=jnp.float32
    )
    total_ref[4 * width : 4 * width + 1, :] += jnp.sum(dnormed * xhat, axis=0, keepdims=True)
    total_ref[4 * width + 8 : 4 * width + 9, :] += jnp.sum(dnormed, axis=0, keepdims=True)
    g = dnormed * gain_ref[...]
    grad = (
        g
        - jnp.mean(g, axis=1, keepdims=True)
        - xhat * jnp.mean(g * xhat, axis=1, keepdims=True)
    ) * inverse
    grad_ref[...] = grad.astype(jnp.bfloat16).reshape(grad_ref.shape)

    @pl.when(step == pl.num_programs(0) - 1)
    def _():
        order = lane_order(True)
        for kind in range(2):
            plain = jnp.dot(
                wgrad_ref[:, 256 * kind : 256 * kind + 256],
                order,
                precision=lax.Precision.HIGHEST,
                preferred_element_type=jnp.float32,
            )
            for side in range(2):
                at = (2 * side + kind) * width
                total_ref[at : at + width, :] = plain[:, 128 * side : 128 * side + 128]


def post(pair, back, gain, bias, ordered, total_rows):
    rows, cols, width = pair.shape
    tile = pl.BlockSpec((STEP_ROWS, cols, width), lambda i: (i, 0, 0))
    whole = lambda *shape: pl.BlockSpec(shape, lambda i: (0,) * len(shape))
    return pl.pallas_call(
        post_kernel,
        grid=(rows // STEP_ROWS,),
        in_specs=[
            tile,
            pl.BlockSpec((STEP_ROWS, cols, 2 * width), lambda i: (i, 0, 0)),
            whole(1, width),
            whole(1, width),
            whole(*ordered.shape),
        ],
        out_specs=[tile, whole(total_rows, width)],
        out_shape=[
            jax.ShapeDtypeStruct(pair.shape, jnp.bfloat16),
            jax.ShapeDtypeStruct((total_rows, width), jnp.float32),
        ],
        scratch_shapes=[pltpu.VMEM(ordered.shape, jnp.float32)],
        compiler_params=pltpu.CompilerParams(vmem_limit_bytes=VMEM_LIMIT),
        cost_estimate=pl.CostEstimate(
            flops=6 * rows * cols * width * 512, bytes_accessed=20 << 20, transcendentals=1 << 20
        ),
        name="input_gradients",
    )(pair, back, gain, bias, ordered)


def product_kernel(half, slab_ref, sides_hbm, *refs):
    block_hbm = refs[:SLABS]
    out_hbm, sides, blocks, out, grads, sems, out_sems = refs[SLABS + half :]
    here = pl.ds(2 * half, 2)
    loads = [
        pltpu.make_async_copy(ref, blocks.at[n], sems.at[n]) for n, ref in enumerate(block_hbm)
    ]
    loads.append(pltpu.make_async_copy(sides_hbm.at[:, here], sides, sems.at[SLABS]))
    for load in loads:
        load.start()

    def place(channel, offset, piece):
        where = lax.rem(slab_ref[0] + offset, SLABS)
        for x in range(2):
            rows = pl.ds(pl.multiple_of(512 * x + 64 * where, 64), 64)
            for r in range(8):
                grads[channel, rows, 128 * r : 128 * r + 128] = jnp.concatenate(
                    [piece(4 * r + 2 * x), piece(4 * r + 2 * x + 1)], axis=0
                )

    def whole(channel, side):
        return jnp.concatenate(
            [
                jnp.concatenate([sides[4 * r + c, side, channel] for c in range(4)], axis=0)
                for r in range(8)
            ],
            axis=1,
        )

    for n, offset in enumerate((0, 7, 1, 6, 2, 5, 3, 4)):
        loads[n].wait()
        for channel in range(2):
            place(channel, offset, lambda d: blocks[n, d, channel])
    loads[SLABS].wait()
    stores = []
    for channel in range(2):
        first = jnp.dot(whole(channel, 1), grads[channel], preferred_element_type=jnp.float32)
        second = lax.dot_general(
            whole(channel, 0),
            grads[channel],
            (((1,), (1,)), ((), ())),
            preferred_element_type=jnp.float32,
        )
        for side, value in enumerate((first, second)):
            value = value.astype(jnp.bfloat16)
            for r in range(8):
                for c in range(4):
                    out[channel, 4 * r + c, side] = value[
                        32 * c : 32 * c + 32, 128 * r : 128 * r + 128
                    ]
        stores.append(
            pltpu.make_async_copy(
                out.at[channel], out_hbm.at[:, here, channel], out_sems.at[channel]
            )
        )
        stores[-1].start()
    for store in stores:
        store.wait()


def products(slab, sides, half, blocks, earlier=None):
    groups, pairs, depth, width = sides.shape
    channels = pairs // 4
    sides = sides.reshape(groups, 4, channels, depth, width)
    operands = [slab, sides, *blocks] + ([] if earlier is None else [earlier])
    bf16 = lambda *shape: pltpu.VMEM(shape, jnp.bfloat16)
    return pl.pallas_call(
        functools.partial(product_kernel, half),
        in_specs=[pl.BlockSpec(memory_space=pltpu.SMEM)]
        + [pl.BlockSpec(memory_space=pltpu.HBM)] * (len(operands) - 1),
        out_specs=pl.BlockSpec(memory_space=pltpu.HBM),
        out_shape=jax.ShapeDtypeStruct(sides.shape, jnp.bfloat16),
        scratch_shapes=[
            bf16(groups, 2, channels, depth, width),
            bf16(SLABS, groups, channels, depth, width),
            bf16(channels, groups, 2, depth, width),
            bf16(channels, 1024, 1024),
            pltpu.SemaphoreType.DMA((SLABS + 1,)),
            pltpu.SemaphoreType.DMA((2,)),
        ],
        input_output_aliases={} if earlier is None else {len(operands) - 1: 0},
        compiler_params=pltpu.CompilerParams(vmem_limit_bytes=PRODUCT_LIMIT),
        cost_estimate=pl.CostEstimate(
            flops=4 * channels * 128 * 1024 * 1024, bytes_accessed=12 << 20, transcendentals=0
        ),
        name="triangle_products",
    )(*operands)


def sum_of_all(x):
    me = lax.axis_index("c")
    swap = lambda x: lax.ppermute(x, "c", [(0, 1), (1, 0)])
    mine = lax.dynamic_index_in_dim(x, me, 0, keepdims=False)
    others = lax.dynamic_index_in_dim(x, 1 - me, 0, keepdims=False)
    part = jnp.sum(all_to_all(mine + swap(others), CHIPS), axis=0)
    part = jnp.sum(all_to_all(jnp.broadcast_to(part, (SLABS,) + part.shape), "z"), axis=0)
    mine = all_to_all(jnp.broadcast_to(part, x.shape[1:]), CHIPS)
    others = swap(mine)
    first = me == 0
    return jnp.stack([jnp.where(first, mine, others), jnp.where(first, others, mine)])


def per_device(pair, layernorm_gain, layernorm_bias, proj_weight, product_grad):
    rows, cols, width = pair.shape
    barrier = lax.optimization_barrier
    split = lambda x: jnp.transpose(x, (2, 1, 0)).reshape(GROUPS, -1, cols, rows)
    join = lambda x: jnp.transpose(x.reshape(-1, cols, rows), (2, 1, 0))
    gain = layernorm_gain.reshape(1, width)
    bias = layernorm_bias.reshape(1, width)
    slab = lax.axis_index("z").astype(jnp.int32).reshape(1)
    both = lambda pair_of: (shift(pair_of[0], 1), shift(pair_of[1], -1))

    after = lambda wanted, done: barrier((wanted, done))[0]
    own = all_to_all(split(product_grad), PLANE)
    sides, ordered = pre(pair, gain, bias, proj_weight)
    a0, b0, sides = barrier((own[:, :2], own[:, 2:], split(sides)))
    sides = all_to_all(sides, PLANE)
    a1 = both((a0, a0))
    b1 = both((b0, b0))
    a1 = barrier(a1)
    a2 = both(a1)
    b1 = after(b1, a1)
    b2 = both(b1)
    a2 = after(a2, b1)
    a3 = both(a2)
    b2 = after(b2, a2)
    b3 = both(b2)
    a3 = after(a3, b2)
    a4 = shift(a3[0], 1)
    b3 = after(b3, a3)
    b4 = shift(b3[1], -1)
    back = products(slab, sides, 0, [a0, *a1, *a2, *a3, a4])
    back = products(slab, sides, 1, [b0, *b1, *b2, *b3, b4], back)
    back = all_to_all(back.reshape(sides.shape), PLANE)

    total_rows = 24 * GROUPS
    pairwise_gradient, total = post(
        pair, join(back), gain, bias, ordered, total_rows
    )
    total = sum_of_all(total.reshape(2, 16, 24, width)) / (rows * 8)
    total = total.reshape(total_rows, width)
    proj_grad = jnp.transpose(total[: 4 * width].reshape(4, width, width), (1, 0, 2))
    proj_grad = proj_grad.reshape(width, 4 * width)
    layernorm_gradient = jnp.stack([total[4 * width], total[4 * width + 8]])
    return pairwise_gradient, proj_grad, layernorm_gradient


def solution(mesh):
    fine = Mesh(mesh.devices.reshape(4, 2, 2, 8, 2), ("y", "xh", "xl", "z", "c"))
    tiles = P(("y", "xh"), ("xl", "z", "c"), None)
    return jax.shard_map(
        per_device,
        mesh=fine,
        in_specs=(tiles, P(), P(), P(), tiles),
        out_specs=(tiles, P(), P()),
        check_vma=False,
    )
```

```python
import functools

import jax
import jax.numpy as jnp
from jax import lax
from jax.experimental import pallas as pl
from jax.experimental.pallas import tpu as pltpu
from jax.sharding import Mesh, PartitionSpec as P

PLANE = ("y", "xh", "xl", "c")
GROUPS = 32
SLABS = 8
STEP_ROWS = 64
VMEM_LIMIT = 32 * 1024 * 1024
PRODUCT_LIMIT = 58 * 1024 * 1024


def all_to_all(x, axes):
    return lax.all_to_all(x, axes, split_axis=0, concat_axis=0, tiled=True)


def shift(x, by):
    return lax.ppermute(x, "z", [(i, (i + by) % SLABS) for i in range(SLABS)])


def normalize(pair_ref, gain_ref, bias_ref):
    x = pair_ref[...].astype(jnp.float32)
    x = x.reshape(x.shape[0] * x.shape[1], x.shape[2])
    centred = x - jnp.mean(x, axis=1, keepdims=True)
    inverse = lax.rsqrt(jnp.mean(centred * centred, axis=1, keepdims=True) + 1e-05)
    xhat = centred * inverse
    normed = (xhat * gain_ref[...] + bias_ref[...]).astype(jnp.bfloat16)
    return xhat, inverse, normed


def lane_order(transposed):
    source = lax.broadcasted_iota(jnp.int32, (256, 256), 1 if transposed else 0)
    lane = lax.broadcasted_iota(jnp.int32, (256, 256), 0 if transposed else 1)
    side, half = (lane >> 1) & 1, (lane >> 2) & 1
    wanted = side * 128 + (lane >> 3) * 4 + half * 2 + (lane & 1)
    return jnp.where(source == wanted, 1.0, 0.0).astype(jnp.float32)


def pre_kernel(pair_ref, gain_ref, bias_ref, weight_ref, sides_ref, ordered_ref):
    @pl.when(pl.program_id(0) == 0)
    def _():
        order = lane_order(False).astype(jnp.bfloat16)
        for kind in range(2):
            plain = jnp.concatenate(
                [weight_ref[:, at : at + 128] for at in (128 * kind, 256 + 128 * kind)], axis=1
            )
            ordered_ref[:, 256 * kind : 256 * kind + 256] = jnp.dot(
                plain, order, preferred_element_type=jnp.float32
            ).astype(jnp.bfloat16)

    _, _, normed = normalize(pair_ref, gain_ref, bias_ref)
    proj = jnp.dot(normed, ordered_ref[...], preferred_element_type=jnp.float32)
    sides = jax.nn.sigmoid(proj[:, 256:]) * proj[:, :256]
    sides_ref[...] = sides.astype(jnp.bfloat16).reshape(sides_ref.shape)


def pre(pair, gain, bias, weight):
    rows, cols, width = pair.shape
    tile = pl.BlockSpec((STEP_ROWS, cols, width), lambda i: (i, 0, 0))
    whole = lambda *shape: pl.BlockSpec(shape, lambda i: (0,) * len(shape))
    return pl.pallas_call(
        pre_kernel,
        grid=(rows // STEP_ROWS,),
        in_specs=[tile, whole(1, width), whole(1, width), whole(*weight.shape)],
        out_specs=[
            pl.BlockSpec((STEP_ROWS, cols, 2 * width), lambda i: (i, 0, 0)),
            whole(*weight.shape),
        ],
        out_shape=[
            jax.ShapeDtypeStruct((rows, cols, 2 * width), jnp.bfloat16),
            jax.ShapeDtypeStruct(weight.shape, jnp.bfloat16),
        ],
        compiler_params=pltpu.CompilerParams(vmem_limit_bytes=VMEM_LIMIT),
        cost_estimate=pl.CostEstimate(
            flops=2 * rows * cols * width * 512, bytes_accessed=12 << 20, transcendentals=1 << 20
        ),
        name="gated_projections",
    )(pair, gain, bias, weight)


def post_kernel(
    pair_ref, back_ref, gain_ref, bias_ref, ordered_ref, grad_ref, total_ref, wgrad_ref
):
    step = pl.program_id(0)

    @pl.when(step == 0)
    def _():
        total_ref[...] = jnp.zeros_like(total_ref)
        wgrad_ref[...] = jnp.zeros_like(wgrad_ref)

    xhat, inverse, normed = normalize(pair_ref, gain_ref, bias_ref)
    proj = jnp.dot(normed, ordered_ref[...], preferred_element_type=jnp.float32)
    width = xhat.shape[1]
    value, gate = proj[:, :256], jax.nn.sigmoid(proj[:, 256:])
    gated = back_ref[...].astype(jnp.float32).reshape(gate.shape) * gate
    dproj = jnp.concatenate(
        [gated.astype(jnp.bfloat16), (gated * value * (1.0 - gate)).astype(jnp.bfloat16)], axis=1
    )
    dnormed = lax.dot_general(
        dproj, ordered_ref[...], (((1,), (1,)), ((), ())), preferred_element_type=jnp.float32
    )
    wgrad_ref[...] += lax.dot_general(
        normed, dproj, (((0,), (0,)), ((), ())), preferred_element_type=jnp.float32
    )
    total_ref[4 * width : 4 * width + 1, :] += jnp.sum(dnormed * xhat, axis=0, keepdims=True)
    total_ref[4 * width + 8 : 4 * width + 9, :] += jnp.sum(dnormed, axis=0, keepdims=True)
    g = dnormed * gain_ref[...]
    grad = (
        g
        - jnp.mean(g, axis=1, keepdims=True)
        - xhat * jnp.mean(g * xhat, axis=1, keepdims=True)
    ) * inverse
    grad_ref[...] = grad.astype(jnp.bfloat16).reshape(grad_ref.shape)

    @pl.when(step == pl.num_programs(0) - 1)
    def _():
        order = lane_order(True)
        for kind in range(2):
            plain = jnp.dot(
                wgrad_ref[:, 256 * kind : 256 * kind + 256],
                order,
                precision=lax.Precision.HIGHEST,
                preferred_element_type=jnp.float32,
            )
            for side in range(2):
                at = (2 * side + kind) * width
                total_ref[at : at + width, :] = plain[:, 128 * side : 128 * side + 128]


def post(pair, back, gain, bias, ordered, total_rows):
    rows, cols, width = pair.shape
    tile = pl.BlockSpec((STEP_ROWS, cols, width), lambda i: (i, 0, 0))
    whole = lambda *shape: pl.BlockSpec(shape, lambda i: (0,) * len(shape))
    return pl.pallas_call(
        post_kernel,
        grid=(rows // STEP_ROWS,),
        in_specs=[
            tile,
            pl.BlockSpec((STEP_ROWS, cols, 2 * width), lambda i: (i, 0, 0)),
            whole(1, width),
            whole(1, width),
            whole(*ordered.shape),
        ],
        out_specs=[tile, whole(total_rows, width)],
        out_shape=[
            jax.ShapeDtypeStruct(pair.shape, jnp.bfloat16),
            jax.ShapeDtypeStruct((total_rows, width), jnp.float32),
        ],
        scratch_shapes=[pltpu.VMEM(ordered.shape, jnp.float32)],
        compiler_params=pltpu.CompilerParams(vmem_limit_bytes=VMEM_LIMIT),
        cost_estimate=pl.CostEstimate(
            flops=6 * rows * cols * width * 512, bytes_accessed=20 << 20, transcendentals=1 << 20
        ),
        name="input_gradients",
    )(pair, back, gain, bias, ordered)


def product_kernel(half, slab_ref, sides_hbm, *refs):
    block_hbm = refs[:SLABS]
    out_hbm, sides, blocks, out, grads, sems, out_sems = refs[SLABS + half :]
    here = pl.ds(2 * half, 2)
    loads = [
        pltpu.make_async_copy(ref, blocks.at[n], sems.at[n]) for n, ref in enumerate(block_hbm)
    ]
    loads.append(pltpu.make_async_copy(sides_hbm.at[:, here], sides, sems.at[SLABS]))
    for load in loads:
        load.start()

    def place(channel, offset, piece):
        where = lax.rem(slab_ref[0] + offset, SLABS)
        for x in range(2):
            rows = pl.ds(pl.multiple_of(512 * x + 64 * where, 64), 64)
            for r in range(8):
                grads[channel, rows, 128 * r : 128 * r + 128] = jnp.concatenate(
                    [piece(4 * r + 2 * x), piece(4 * r + 2 * x + 1)], axis=0
                )

    def whole(channel, side):
        return jnp.concatenate(
            [
                jnp.concatenate([sides[4 * r + c, side, channel] for c in range(4)], axis=0)
                for r in range(8)
            ],
            axis=1,
        )

    for n, offset in enumerate((0, 7, 1, 6, 2, 5, 3, 4)):
        loads[n].wait()
        for channel in range(2):
            place(channel, offset, lambda d: blocks[n, d, channel])
    loads[SLABS].wait()
    stores = []
    for channel in range(2):
        first = jnp.dot(whole(channel, 1), grads[channel], preferred_element_type=jnp.float32)
        second = lax.dot_general(
            whole(channel, 0),
            grads[channel],
            (((1,), (1,)), ((), ())),
            preferred_element_type=jnp.float32,
        )
        for side, value in enumerate((first, second)):
            value = value.astype(jnp.bfloat16)
            for r in range(8):
                for c in range(4):
                    out[channel, 4 * r + c, side] = value[
                        32 * c : 32 * c + 32, 128 * r : 128 * r + 128
                    ]
        stores.append(
            pltpu.make_async_copy(
                out.at[channel], out_hbm.at[:, here, channel], out_sems.at[channel]
            )
        )
        stores[-1].start()
    for store in stores:
        store.wait()


def products(slab, sides, half, blocks, earlier=None):
    groups, pairs, depth, width = sides.shape
    channels = pairs // 4
    sides = sides.reshape(groups, 4, channels, depth, width)
    operands = [slab, sides, *blocks] + ([] if earlier is None else [earlier])
    bf16 = lambda *shape: pltpu.VMEM(shape, jnp.bfloat16)
    return pl.pallas_call(
        functools.partial(product_kernel, half),
        in_specs=[pl.BlockSpec(memory_space=pltpu.SMEM)]
        + [pl.BlockSpec(memory_space=pltpu.HBM)] * (len(operands) - 1),
        out_specs=pl.BlockSpec(memory_space=pltpu.HBM),
        out_shape=jax.ShapeDtypeStruct(sides.shape, jnp.bfloat16),
        scratch_shapes=[
            bf16(groups, 2, channels, depth, width),
            bf16(SLABS, groups, channels, depth, width),
            bf16(channels, groups, 2, depth, width),
            bf16(channels, 1024, 1024),
            pltpu.SemaphoreType.DMA((SLABS + 1,)),
            pltpu.SemaphoreType.DMA((2,)),
        ],
        input_output_aliases={} if earlier is None else {len(operands) - 1: 0},
        compiler_params=pltpu.CompilerParams(vmem_limit_bytes=PRODUCT_LIMIT),
        cost_estimate=pl.CostEstimate(
            flops=4 * channels * 128 * 1024 * 1024, bytes_accessed=12 << 20, transcendentals=0
        ),
        name="triangle_products",
    )(*operands)


def sum_of_all(x):
    part = jnp.sum(all_to_all(x, PLANE), axis=0)
    part = jnp.sum(all_to_all(jnp.broadcast_to(part, (SLABS,) + part.shape), "z"), axis=0)
    return all_to_all(jnp.broadcast_to(part, x.shape), PLANE)


def per_device(pair, layernorm_gain, layernorm_bias, proj_weight, product_grad):
    rows, cols, width = pair.shape
    barrier = lax.optimization_barrier
    split = lambda x: jnp.transpose(x, (2, 1, 0)).reshape(GROUPS, -1, cols, rows)
    join = lambda x: jnp.transpose(x.reshape(-1, cols, rows), (2, 1, 0))
    gain = layernorm_gain.reshape(1, width)
    bias = layernorm_bias.reshape(1, width)
    slab = lax.axis_index("z").astype(jnp.int32).reshape(1)
    both = lambda pair_of: (shift(pair_of[0], 1), shift(pair_of[1], -1))

    after = lambda wanted, done: barrier((wanted, done))[0]
    own = all_to_all(split(product_grad), PLANE)
    sides, ordered = pre(pair, gain, bias, proj_weight)
    a0, b0, sides = barrier((own[:, :2], own[:, 2:], split(sides)))
    sides = all_to_all(sides, PLANE)
    a1 = both((a0, a0))
    b1 = both((b0, b0))
    a1 = barrier(a1)
    a2 = both(a1)
    b1 = after(b1, a1)
    b2 = both(b1)
    a2 = after(a2, b1)
    a3 = both(a2)
    b2 = after(b2, a2)
    b3 = both(b2)
    a3 = after(a3, b2)
    a4 = shift(a3[0], 1)
    b3 = after(b3, a3)
    b4 = shift(b3[1], -1)
    back = products(slab, sides, 0, [a0, *a1, *a2, *a3, a4])
    back = products(slab, sides, 1, [b0, *b1, *b2, *b3, b4], back)
    back = all_to_all(back.reshape(sides.shape), PLANE)

    total_rows = 24 * GROUPS
    pairwise_gradient, total = post(
        pair, join(back), gain, bias, ordered, total_rows
    )
    total = sum_of_all(total.reshape(GROUPS, 24, width)) / (rows * 8)
    total = total.reshape(total_rows, width)
    proj_grad = jnp.transpose(total[: 4 * width].reshape(4, width, width), (1, 0, 2))
    proj_grad = proj_grad.reshape(width, 4 * width)
    layernorm_gradient = jnp.stack([total[4 * width], total[4 * width + 8]])
    return pairwise_gradient, proj_grad, layernorm_gradient


def solution(mesh):
    fine = Mesh(mesh.devices.reshape(4, 2, 2, 8, 2), ("y", "xh", "xl", "z", "c"))
    tiles = P(("y", "xh"), ("xl", "z", "c"), None)
    return jax.shard_map(
        per_device,
        mesh=fine,
        in_specs=(tiles, P(), P(), P(), tiles),
        out_specs=(tiles, P(), P()),
        check_vma=False,
    )
```

```python
import functools

import jax
import jax.numpy as jnp
from jax import lax
from jax.experimental import pallas as pl
from jax.experimental.pallas import tpu as pltpu
from jax.sharding import Mesh, PartitionSpec as P

PLANE = ("y", "xh", "xl", "c")
CHIPS = ("y", "xh", "xl")
GROUPS = 32
SLABS = 8
OFFSETS = (0, 7, 1, 6, 2, 5, 3, 4)
STEP_ROWS = 64
VMEM_LIMIT = 32 * 1024 * 1024
PRODUCT_LIMIT = 58 * 1024 * 1024


def all_to_all(x, axes):
    return lax.all_to_all(x, axes, split_axis=0, concat_axis=0, tiled=True)


def shift(x, by):
    return lax.ppermute(x, "z", [(i, (i + by) % SLABS) for i in range(SLABS)])


def normalize(pair_ref, gain_ref, bias_ref):
    x = pair_ref[...].astype(jnp.float32)
    x = x.reshape(x.shape[0] * x.shape[1], x.shape[2])
    centred = x - jnp.mean(x, axis=1, keepdims=True)
    inverse = lax.rsqrt(jnp.mean(centred * centred, axis=1, keepdims=True) + 1e-05)
    xhat = centred * inverse
    normed = (xhat * gain_ref[...] + bias_ref[...]).astype(jnp.bfloat16)
    return xhat, inverse, normed


def lane_order(transposed):
    source = lax.broadcasted_iota(jnp.int32, (256, 256), 1 if transposed else 0)
    lane = lax.broadcasted_iota(jnp.int32, (256, 256), 0 if transposed else 1)
    side, half = (lane >> 1) & 1, (lane >> 2) & 1
    wanted = side * 128 + (lane >> 3) * 4 + half * 2 + (lane & 1)
    return jnp.where(source == wanted, 1.0, 0.0).astype(jnp.float32)


def pre_kernel(pair_ref, gain_ref, bias_ref, weight_ref, sides_ref, ordered_ref):
    @pl.when(pl.program_id(0) == 0)
    def _():
        order = lane_order(False).astype(jnp.bfloat16)
        for kind in range(2):
            plain = jnp.concatenate(
                [weight_ref[:, at : at + 128] for at in (128 * kind, 256 + 128 * kind)], axis=1
            )
            ordered_ref[:, 256 * kind : 256 * kind + 256] = jnp.dot(
                plain, order, preferred_element_type=jnp.float32
            ).astype(jnp.bfloat16)

    _, _, normed = normalize(pair_ref, gain_ref, bias_ref)
    proj = jnp.dot(normed, ordered_ref[...], preferred_element_type=jnp.float32)
    sides = jax.nn.sigmoid(proj[:, 256:]) * proj[:, :256]
    sides_ref[...] = sides.astype(jnp.bfloat16).reshape(sides_ref.shape)


def pre(pair, gain, bias, weight):
    rows, cols, width = pair.shape
    tile = pl.BlockSpec((STEP_ROWS, cols, width), lambda i: (i, 0, 0))
    whole = lambda *shape: pl.BlockSpec(shape, lambda i: (0,) * len(shape))
    return pl.pallas_call(
        pre_kernel,
        grid=(rows // STEP_ROWS,),
        in_specs=[tile, whole(1, width), whole(1, width), whole(*weight.shape)],
        out_specs=[
            pl.BlockSpec((STEP_ROWS, cols, 2 * width), lambda i: (i, 0, 0)),
            whole(*weight.shape),
        ],
        out_shape=[
            jax.ShapeDtypeStruct((rows, cols, 2 * width), jnp.bfloat16),
            jax.ShapeDtypeStruct(weight.shape, jnp.bfloat16),
        ],
        compiler_params=pltpu.CompilerParams(vmem_limit_bytes=VMEM_LIMIT),
        cost_estimate=pl.CostEstimate(
            flops=2 * rows * cols * width * 512, bytes_accessed=12 << 20, transcendentals=1 << 20
        ),
        name="gated_projections",
    )(pair, gain, bias, weight)


def post_kernel(
    pair_ref, back_ref, gain_ref, bias_ref, ordered_ref, grad_ref, total_ref, wgrad_ref
):
    step = pl.program_id(0)

    @pl.when(step == 0)
    def _():
        total_ref[...] = jnp.zeros_like(total_ref)
        wgrad_ref[...] = jnp.zeros_like(wgrad_ref)

    xhat, inverse, normed = normalize(pair_ref, gain_ref, bias_ref)
    proj = jnp.dot(normed, ordered_ref[...], preferred_element_type=jnp.float32)
    width = xhat.shape[1]
    value, gate = proj[:, :256], jax.nn.sigmoid(proj[:, 256:])
    gated = back_ref[...].astype(jnp.float32).reshape(gate.shape) * gate
    dproj = jnp.concatenate(
        [gated.astype(jnp.bfloat16), (gated * value * (1.0 - gate)).astype(jnp.bfloat16)], axis=1
    )
    dnormed = lax.dot_general(
        dproj, ordered_ref[...], (((1,), (1,)), ((), ())), preferred_element_type=jnp.float32
    )
    wgrad_ref[...] += lax.dot_general(
        normed, dproj, (((0,), (0,)), ((), ())), preferred_element_type=jnp.float32
    )
    total_ref[4 * width : 4 * width + 1, :] += jnp.sum(dnormed * xhat, axis=0, keepdims=True)
    total_ref[4 * width + 8 : 4 * width + 9, :] += jnp.sum(dnormed, axis=0, keepdims=True)
    g = dnormed * gain_ref[...]
    grad = (
        g
        - jnp.mean(g, axis=1, keepdims=True)
        - xhat * jnp.mean(g * xhat, axis=1, keepdims=True)
    ) * inverse
    grad_ref[...] = grad.astype(jnp.bfloat16).reshape(grad_ref.shape)

    @pl.when(step == pl.num_programs(0) - 1)
    def _():
        order = lane_order(True)
        for kind in range(2):
            plain = jnp.dot(
                wgrad_ref[:, 256 * kind : 256 * kind + 256],
                order,
                precision=lax.Precision.HIGHEST,
                preferred_element_type=jnp.float32,
            )
            for side in range(2):
                at = (2 * side + kind) * width
                total_ref[at : at + width, :] = plain[:, 128 * side : 128 * side + 128]


def post(pair, back, gain, bias, ordered, total_rows):
    rows, cols, width = pair.shape
    tile = pl.BlockSpec((STEP_ROWS, cols, width), lambda i: (i, 0, 0))
    whole = lambda *shape: pl.BlockSpec(shape, lambda i: (0,) * len(shape))
    return pl.pallas_call(
        post_kernel,
        grid=(rows // STEP_ROWS,),
        in_specs=[
            tile,
            pl.BlockSpec((STEP_ROWS, cols, 2 * width), lambda i: (i, 0, 0)),
            whole(1, width),
            whole(1, width),
            whole(*ordered.shape),
        ],
        out_specs=[tile, whole(total_rows, width)],
        out_shape=[
            jax.ShapeDtypeStruct(pair.shape, jnp.bfloat16),
            jax.ShapeDtypeStruct((total_rows, width), jnp.float32),
        ],
        scratch_shapes=[pltpu.VMEM(ordered.shape, jnp.float32)],
        compiler_params=pltpu.CompilerParams(vmem_limit_bytes=VMEM_LIMIT),
        cost_estimate=pl.CostEstimate(
            flops=6 * rows * cols * width * 512, bytes_accessed=20 << 20, transcendentals=1 << 20
        ),
        name="input_gradients",
    )(pair, back, gain, bias, ordered)


def product_kernel(slab_ref, sides_hbm, *refs):
    block_hbm = refs[: 2 * SLABS]
    out_hbm, sides, blocks, out, grads, sems, side_sems, out_sems = refs[2 * SLABS :]
    loads = [
        pltpu.make_async_copy(ref, blocks.at[n], sems.at[n]) for n, ref in enumerate(block_hbm)
    ]
    side_loads = [
        pltpu.make_async_copy(
            sides_hbm.at[:, pl.ds(2 * half, 2)], sides.at[half], side_sems.at[half]
        )
        for half in range(2)
    ]
    for half in range(2):
        for load in loads[SLABS * half : SLABS * half + SLABS]:
            load.start()
        side_loads[half].start()

    def place(channel, n):
        where = lax.rem(slab_ref[0] + OFFSETS[n % SLABS], SLABS)
        for x in range(2):
            rows = pl.ds(pl.multiple_of(512 * x + 64 * where, 64), 64)
            for r in range(8):
                grads[channel, rows, 128 * r : 128 * r + 128] = jnp.concatenate(
                    [blocks[n, 4 * r + 2 * x, channel], blocks[n, 4 * r + 2 * x + 1, channel]],
                    axis=0,
                )

    def whole(half, channel, side):
        return jnp.concatenate(
            [
                jnp.concatenate(
                    [sides[half, 4 * r + c, side, channel] for c in range(4)], axis=0
                )
                for r in range(8)
            ],
            axis=1,
        )

    stores = []
    for half in range(2):
        for n in range(SLABS * half, SLABS * half + SLABS):
            loads[n].wait()
            for channel in range(2):
                place(channel, n)
        side_loads[half].wait()
        for channel in range(2):
            first = jnp.dot(
                whole(half, channel, 1), grads[channel], preferred_element_type=jnp.float32
            )
            second = lax.dot_general(
                whole(half, channel, 0),
                grads[channel],
                (((1,), (1,)), ((), ())),
                preferred_element_type=jnp.float32,
            )
            at = 2 * half + channel
            for side, value in enumerate((first, second)):
                value = value.astype(jnp.bfloat16)
                for r in range(8):
                    for c in range(4):
                        out[at, 4 * r + c, side] = value[
                            32 * c : 32 * c + 32, 128 * r : 128 * r + 128
                        ]
            stores.append(
                pltpu.make_async_copy(
                    out.at[at], out_hbm.at[:, pl.ds(2 * half, 2), channel], out_sems.at[at]
                )
            )
            stores[-1].start()
    for store in stores:
        store.wait()


def products(slab, sides, blocks):
    groups, pairs, depth, width = sides.shape
    channels = pairs // 4
    sides = sides.reshape(groups, 4, channels, depth, width)
    bf16 = lambda *shape: pltpu.VMEM(shape, jnp.bfloat16)
    out = pl.pallas_call(
        product_kernel,
        in_specs=[pl.BlockSpec(memory_space=pltpu.SMEM)]
        + [pl.BlockSpec(memory_space=pl.ANY)] * (1 + len(blocks)),
        out_specs=pl.BlockSpec(memory_space=pl.ANY),
        out_shape=jax.ShapeDtypeStruct(sides.shape, jnp.bfloat16),
        scratch_shapes=[
            bf16(2, groups, 2, channels, depth, width),
            bf16(2 * SLABS, groups, channels, depth, width),
            bf16(2 * channels, groups, 2, depth, width),
            bf16(channels, 1024, 1024),
            pltpu.SemaphoreType.DMA((2 * SLABS,)),
            pltpu.SemaphoreType.DMA((2,)),
            pltpu.SemaphoreType.DMA((4,)),
        ],
        compiler_params=pltpu.CompilerParams(vmem_limit_bytes=PRODUCT_LIMIT),
        cost_estimate=pl.CostEstimate(
            flops=16 * 128 * 1024 * 1024, bytes_accessed=12 << 20, transcendentals=0
        ),
        name="triangle_products",
    )(slab, sides, *blocks)
    return out.reshape(groups, pairs, depth, width)


def sum_of_all(x):
    part = jnp.sum(all_to_all(x, PLANE), axis=0)
    part = jnp.sum(all_to_all(jnp.broadcast_to(part, (SLABS,) + part.shape), "z"), axis=0)
    return all_to_all(jnp.broadcast_to(part, x.shape), PLANE)


def per_device(pair, layernorm_gain, layernorm_bias, proj_weight, product_grad):
    rows, cols, width = pair.shape
    barrier = lax.optimization_barrier
    split = lambda x: jnp.transpose(x, (2, 1, 0)).reshape(GROUPS, -1, cols, rows)
    join = lambda x: jnp.transpose(x.reshape(-1, cols, rows), (2, 1, 0))
    gain = layernorm_gain.reshape(1, width)
    bias = layernorm_bias.reshape(1, width)
    slab = lax.axis_index("z").astype(jnp.int32).reshape(1)
    both = lambda pair_of: (shift(pair_of[0], 1), shift(pair_of[1], -1))

    after = lambda wanted, done: barrier((wanted, done))[0]
    own = all_to_all(split(product_grad), PLANE)
    sides, ordered = pre(pair, gain, bias, proj_weight)
    a0, own = barrier((own[:, :2], own))
    b0, sides = barrier((own[:, 2:], split(sides)))
    sides = all_to_all(sides, PLANE)
    a1 = both((a0, a0))
    b1 = both((b0, b0))
    a1 = barrier(a1)
    a2 = both(a1)
    b1 = after(b1, a1)
    b2 = both(b1)
    a2 = after(a2, b1)
    a3 = both(a2)
    b2 = after(b2, a2)
    b3 = both(b2)
    a3 = after(a3, b2)
    a4 = shift(a3[0], 1)
    b3 = after(b3, a3)
    b4 = shift(b3[1], -1)
    blocks = [a0, *a1, *a2, *a3, a4, b0, *b1, *b2, *b3, b4]
    back = all_to_all(products(slab, sides, blocks), PLANE)

    total_rows = 24 * GROUPS
    pairwise_gradient, total = post(
        pair, join(back), gain, bias, ordered, total_rows
    )
    total = sum_of_all(total.reshape(GROUPS, 24, width)) / (rows * 8)
    total = total.reshape(total_rows, width)
    proj_grad = jnp.transpose(total[: 4 * width].reshape(4, width, width), (1, 0, 2))
    proj_grad = proj_grad.reshape(width, 4 * width)
    layernorm_gradient = jnp.stack([total[4 * width], total[4 * width + 8]])
    return pairwise_gradient, proj_grad, layernorm_gradient


def solution(mesh):
    fine = Mesh(mesh.devices.reshape(4, 2, 2, 8, 2), ("y", "xh", "xl", "z", "c"))
    tiles = P(("y", "xh"), ("xl", "z", "c"), None)
    return jax.shard_map(
        per_device,
        mesh=fine,
        in_specs=(tiles, P(), P(), P(), tiles),
        out_specs=(tiles, P(), P()),
        check_vma=False,
    )
```
